128 devices in a mesh: req: 2 (over core), vocab: 64 (over x, y, z).
Axes of the slice: x: 4, y: 4, z: 4, core: 2. Of those that a mesh axis runs over, the one named last changes fastest.
Arguments:
- hidden: bfloat16 [512, 7168], P('req', 'vocab'), may hold values from -6000 to 6000
- next_embedding: bfloat16 [512, 7168], P('req', 'vocab'), may hold values from -6000 to 6000
- final_gain: bfloat16 [7168], P('vocab'), may hold values from 0.5 to 1.5
- hidden_gain: bfloat16 [7168], P('vocab'), may hold values from 0.5 to 1.5
- embed_gain: bfloat16 [7168], P('vocab'), may hold values from 0.5 to 1.5
- draft_gain: bfloat16 [7168], P('vocab'), may hold values from 0.5 to 1.5
- head_weight: bfloat16 [7168, 65536], P(None, 'vocab'), may hold values from -3 to 40
- proj_embed: bfloat16 [7168, 7168], P('vocab'), may hold values from -1 to 4
- proj_hidden: bfloat16 [7168, 7168], P('vocab'), may hold values from -0.1875 to 0.1875
- token_ids: int32 [512], P('req'), may hold values from 0 to 65535
- row_request: int32 [512], P('req'), may hold values from 0 to 63
Outputs:
- main_logprobs: float32 [512, 65536], P('req', 'vocab')
- draft_logprobs: float32 [512, 65536], P('req', 'vocab')
- request_score: float32 [64], replicated
The draws below stay inside these ranges and needn't reach their ends.
All inputs are finite; a program needn't handle non-finite values.
Results may differ from the reference program's by a relative error of at most 0.0036.
Values may be sent and summed in bfloat16 or wider, within the bound.
A program may use at most 128 MiB of HBM per device.

```python
import math
import jax
import jax.numpy as jnp
from jax import lax

D = 7168
VOCAB = 65536
REQS = 64
ROWS = 512


def spike_dims():
    return jnp.arange(4, dtype=jnp.int32) * (D // 4)


def plant_spikes(values, phase):
    positions = jnp.arange(ROWS, dtype=jnp.int32)
    chosen = positions % 16 == phase
    target = spike_dims()[positions // 16 % 4]
    features = jnp.arange(D, dtype=jnp.int32)
    marked = chosen[:, None] & (features[None, :] == target[:, None])
    return jnp.where(marked, 60.0 * math.sqrt(D), values)


def rows_draw(key, phase):
    values = jax.random.truncated_normal(key, -6.0, 6.0, (ROWS, D), jnp.float32)
    values = plant_spikes(values, phase)
    return values.astype(jnp.bfloat16)


def draw_hidden(key, part):
    key = jax.random.fold_in(key, 1)
    return rows_draw(key, 5)


def draw_next_embedding(key, part):
    key = jax.random.fold_in(key, 2)
    return rows_draw(key, 11)


def draw_head_weight(key, part):
    key = jax.random.fold_in(key, 3)
    values = jax.random.truncated_normal(key, -6.0, 6.0, (D, VOCAB), jnp.float32) * (4.0 / math.sqrt(D))
    columns = jax.random.randint(jax.random.fold_in(key, 8), (4,), 0, VOCAB - 1)
    strengths = jnp.array([150.0, 200.0, 260.0, 320.0], jnp.float32) / math.sqrt(D)
    values = values.at[spike_dims(), columns].set(strengths)
    values = values.at[spike_dims(), columns + 1].set(strengths - 2.0 / math.sqrt(D))
    return values.astype(jnp.bfloat16)


def draw_proj_embed(key, part):
    key = jax.random.fold_in(key, 4)
    values = jax.random.truncated_normal(key, -6.0, 6.0, (D, D), jnp.float32) * (1.0 / math.sqrt(D))
    values = values.at[spike_dims(), spike_dims()].add(3.0)
    return values.astype(jnp.bfloat16)


def set_ends(entries, own_key, low, top_value):
    longest = entries.shape.index(max(entries.shape))
    spots = []
    for shift in (0, 1):
        where = [jax.random.randint(jax.random.fold_in(own_key, axis), (), 0, length) for axis, length in enumerate(entries.shape)]
        where[longest] = (where[longest] + shift) % entries.shape[longest]
        spots.append(tuple(where))
    return entries.at[spots[0]].set(low).at[spots[1]].set(top_value)


def spiked(values, stream_key, source, target, parts, factor):
    owner, partner = [(jnp.arange(values.shape[dim]) // (values.shape[dim] // parts)).reshape([-1 if axis == dim else 1 for axis in range(values.ndim)]) for dim in (source, target)]
    chosen = jax.random.permutation(stream_key, parts)[partner]
    strong = (owner == chosen) | (owner == (partner + parts // 2) % parts)
    return jnp.where(strong, factor * values, values)


def block_scale(key, extent, split, low, high):
    def one(axis_at, shards_of):
        heights = jax.random.uniform(jax.random.fold_in(jax.random.fold_in(key, 6), axis_at), (shards_of,), jnp.float32, low / len(split), high / len(split))
        return jnp.repeat(jnp.exp(heights), extent[axis_at] // shards_of).reshape((-1,) + (1,) * (len(extent) - axis_at - 1))

    level = one(*split[0])
    for cut in split[1:]:
        level = level * one(*cut)
    return level


def gaussian_with(key, shape, deviation, bound, cuts, heavy, kind=jnp.bfloat16):
    drawn = deviation * jax.random.normal(key, shape, jnp.float32)
    if cuts:
        drawn = drawn * block_scale(key, shape, cuts, -0.22, 0.18)
    return jnp.clip(spiked(drawn, jax.random.fold_in(key, 3), *heavy), -bound, bound).astype(kind)


def setup_inputs(seed: int = 0) -> dict:
    streams_of = jax.random.split(jax.random.key(seed), 12)
    return {
        "hidden": draw_hidden(jax.random.fold_in(streams_of[11], 71), 0),
        "next_embedding": draw_next_embedding(jax.random.fold_in(streams_of[11], 71), 0),
        "final_gain": jnp.clip(1.0 + 0.1 * jax.random.normal(streams_of[2], (D,), jnp.float32), 0.5, 1.5).astype(jnp.bfloat16),
        "hidden_gain": jnp.clip(1.0 + 0.1 * jax.random.normal(streams_of[3], (D,), jnp.float32), 0.5, 1.5).astype(jnp.bfloat16),
        "embed_gain": jnp.clip(1.0 + 0.1 * jax.random.normal(streams_of[4], (D,), jnp.float32), 0.5, 1.5).astype(jnp.bfloat16),
        "draft_gain": jnp.clip(1.0 + 0.1 * jax.random.normal(streams_of[5], (D,), jnp.float32), 0.5, 1.5).astype(jnp.bfloat16),
        "head_weight": draw_head_weight(jax.random.fold_in(streams_of[11], 71), 0),
        "proj_embed": draw_proj_embed(jax.random.fold_in(streams_of[11], 71), 0),
        "proj_hidden": gaussian_with(streams_of[8], (D, D), D ** -0.5, 0.1875, ((0, 64),), (0, 1, 64, 4.0)),
        "token_ids": set_ends(jax.random.randint(streams_of[9], (ROWS,), 0, VOCAB), jax.random.fold_in(streams_of[9], 1), 0, VOCAB - 1).astype(jnp.int32),
        "row_request": set_ends(jax.random.randint(streams_of[10], (ROWS,), 0, REQS), jax.random.fold_in(streams_of[10], 1), 0, REQS - 1).astype(jnp.int32),
    }


epsilon = 1e-06

def norm_rows(values, gain):
    wide = values.astype(jnp.float32)
    squares = lax.optimization_barrier(jnp.sum(wide * wide, axis=1, keepdims=True))
    return wide * lax.rsqrt(squares / D + epsilon) * gain.astype(jnp.float32)[None, :]

def log_softmax_rows(logits):
    highest = lax.optimization_barrier(jnp.max(logits, axis=1, keepdims=True))
    totals = lax.optimization_barrier(jnp.sum(jnp.exp(logits - highest), axis=1, keepdims=True))
    return logits - (highest + jnp.log(totals))

def reference(hidden, next_embedding, final_gain, hidden_gain, embed_gain, draft_gain, head_weight, proj_embed, proj_hidden, token_ids, row_request):
    normed_final = norm_rows(hidden, final_gain).astype(jnp.bfloat16)
    main_logits = jnp.dot(normed_final, head_weight, preferred_element_type=jnp.float32)
    main_logprobs = log_softmax_rows(main_logits)
    normed_hidden = norm_rows(hidden, hidden_gain).astype(jnp.bfloat16)
    normed_embed = norm_rows(next_embedding, embed_gain).astype(jnp.bfloat16)
    draft_state = jnp.dot(normed_embed, proj_embed, preferred_element_type=jnp.float32) + jnp.dot(normed_hidden, proj_hidden, preferred_element_type=jnp.float32)
    normed_draft = norm_rows(draft_state, draft_gain).astype(jnp.bfloat16)
    draft_logits = jnp.dot(normed_draft, head_weight, preferred_element_type=jnp.float32)
    draft_logprobs = log_softmax_rows(draft_logits)
    picked = jnp.take_along_axis(main_logprobs, token_ids.astype(jnp.int32)[:, None], axis=1)[:, 0]
    request_score = jax.ops.segment_sum(picked, row_request.astype(jnp.int32), num_segments=REQS)
    return (main_logprobs, draft_logprobs, request_score)
```

```python
import jax
import jax.numpy as jnp
from jax import lax
from jax.experimental import pallas as pl
from jax.experimental.pallas import tpu as pltpu
from jax.sharding import PartitionSpec as P

D = 7168
REQS = 64
SIDE = 4
FEAT = 112
ROWS = 256
VOC = 1024
QUART = D // SIDE
HALF = QUART // 2

epsilon = 1e-06
MESH = pl.DeviceIdType.MESH
DMA = pltpu.SemaphoreType.DMA
f32 = jnp.float32
bf16 = jnp.bfloat16
FIRST = (((0,), (0,)), ((), ()))

ORDERS = ((2, 1, 0), (0, 2, 1), (1, 0, 2))
H_PARTS = ((0, 48), (48, 32), (80, 32))
G_PARTS = ((0, 640), (640, 640), (1280, 512))


def coords():
    v = lax.axis_index("vocab")
    return (v // 16, (v // 4) % 4, v % 4)


def device(at, core):
    return (core, (at[0] * 4 + at[1]) * 4 + at[2])


def along(at, axis, step):
    moved = list(at)
    moved[axis] = (at[axis] + step) % 4
    return tuple(moved)


def picks(at, done):
    return tuple(pl.ds(0, 4) if a in done else at[a] for a in range(3))


class Gather:
    def __init__(self, view, order, send, recv, base):
        self.view, self.order, self.send, self.recv, self.base = view, order, send, recv, base

    def copies(self, phase):
        at, core = coords(), lax.axis_index("req")
        axis, done = self.order[phase], self.order[:phase]
        out = []
        for k in (1, 3, 2):
            here = self.view(picks(at, done))
            index = self.base + phase * 3 + k - 1
            out.append(
                pltpu.make_async_remote_copy(
                    src_ref=here,
                    dst_ref=here,
                    send_sem=self.send.at[index],
                    recv_sem=self.recv.at[index],
                    device_id=device(along(at, axis, k), core),
                    device_id_type=MESH,
                )
            )
        return out

    def start(self, phase):
        for copy in self.copies(phase):
            copy.start()

    def wait(self, phase):
        at, core = coords(), lax.axis_index("req")
        axis, done = self.order[phase], self.order[:phase]
        for k in (1, 3, 2):
            source = along(at, axis, 4 - k)
            there = self.view(picks(source, done))
            index = self.base + phase * 3 + k - 1
            pltpu.make_async_remote_copy(
                src_ref=there,
                dst_ref=there,
                send_sem=self.send.at[index],
                recv_sem=self.recv.at[index],
                device_id=device(along(at, axis, k), core),
                device_id_type=MESH,
            ).wait_recv()

    def wait_sends(self):
        for phase in range(3):
            for copy in self.copies(phase):
                copy.wait_send()


def turn(row):
    return jnp.broadcast_to(row, (128, row.shape[1])).T


def kernel(
    hid_ref, emb_ref, gains_ref, token_ref, request_ref, head_ref, pe_ref, ph_ref,
    main_ref, draft_ref, lse_ref, score_ref,
    head, small, gath, xe, xh, we, wh, part, recv, sq, gd, stats, score_buf,
    head_sem, own_sem,
    small_s, small_r, w_s, w_r, x_s, x_r, h_s, h_r, rs_s, rs_r, q_s, q_r, g_s, g_r, st_s, st_r, sc_s, sc_r,
):
    core = lax.axis_index("req")
    at = coords()
    x, y, z = at
    me32 = (x * 4 + y) * 2 + core

    barrier = pltpu.get_barrier_semaphore()

    def greet_plane(i, _):
        peer = (me32 + i) % 32
        pl.semaphore_signal(
            barrier, inc=1, device_id=device((peer // 8, (peer // 2) % 4, z), peer % 2), device_id_type=MESH
        )
        return 0

    lax.fori_loop(1, 32, greet_plane, 0)
    for k in (1, 2, 3):
        for c in (0, 1):
            pl.semaphore_signal(barrier, inc=1, device_id=device(along(at, 2, k), c), device_id_type=MESH)

    head_copies = [
        pltpu.make_async_copy(
            head_ref.at[pl.ds(i * QUART, QUART)], head.at[pl.ds(i * QUART, QUART)], head_sem.at[i]
        )
        for i in range(4)
    ]

    def columns(zz):
        return pl.ds(pl.multiple_of(zz * QUART + core * HALF, 128), HALF)

    own_copies = [
        pltpu.make_async_copy(pe_ref.at[:, columns(z)], we.at[z], own_sem.at[0]),
        pltpu.make_async_copy(ph_ref.at[:, columns(z)], wh.at[z], own_sem.at[1]),
    ]
    for copy in own_copies:
        copy.start()
    for copy in head_copies:
        copy.start()

    hid = hid_ref[...].astype(f32)
    emb = emb_ref[...].astype(f32)
    gains = gains_ref[...]
    block = jnp.concatenate(
        [
            jnp.sum(hid * hid, axis=0, keepdims=True),
            jnp.sum(emb * emb, axis=0, keepdims=True),
            jnp.concatenate([gains[3:4], gains[3:4]], axis=1),
            jnp.zeros((5, ROWS), f32),
        ],
        axis=0,
    )
    small[x, y, z] = block
    pl.semaphore_wait(barrier, 37)

    small_gather = Gather(lambda s: small.at[s], (2, 1, 0), small_s, small_r, 0)
    small_gather.start(0)

    def w_copies(k):
        to = along(at, 2, k)
        return [
            pltpu.make_async_remote_copy(
                src_ref=src.at[:, columns(to[2])],
                dst_ref=dst.at[z],
                send_sem=w_s.at[j, k - 1],
                recv_sem=w_r.at[j, k - 1],
                device_id=device(to, core),
                device_id_type=MESH,
            )
            for j, (src, dst) in enumerate(((pe_ref, we), (ph_ref, wh)))
        ]

    for k in (1, 3, 2):
        for copy in w_copies(k):
            copy.start()

    small_gather.wait(0)
    small_gather.start(1)
    final_gain = turn(gains[0:1])[:FEAT, :1]
    hidden_gain = turn(gains[1:2])[:FEAT, :1]
    embed_gain = turn(gains[2:3])[:FEAT, :1]
    small_gather.wait(1)
    small_gather.start(2)
    small_gather.wait(2)

    squares = jnp.sum(small[...].reshape(64, 8, ROWS), axis=0)
    hid_scale = lax.rsqrt(squares[0:1] / D + epsilon)
    emb_scale = lax.rsqrt(squares[1:2] / D + epsilon)
    gath[x, y, z] = (hid * hid_scale * final_gain).astype(bf16)
    mine = pl.ds(pl.multiple_of(core * ROWS, 128), ROWS)
    xe[z, :, mine] = (emb * emb_scale * embed_gain).astype(bf16)
    xh[z, :, mine] = (hid * hid_scale * hidden_gain).astype(bf16)

    def x_copies():
        out = []
        for k in range(4):
            for dc in (0, 1):
                if k == 0 and dc == 0:
                    continue
                for j, buf in enumerate((xe, xh)):
                    out.append(
                        pltpu.make_async_remote_copy(
                            src_ref=buf.at[z, :, mine],
                            dst_ref=buf.at[z, :, mine],
                            send_sem=x_s.at[j, k * 2 + dc],
                            recv_sem=x_r.at[j, k * 2 + dc],
                            device_id=device(along(at, 2, k), (core + dc) % 2),
                            device_id_type=MESH,
                        )
                    )
        return out

    def x_waits():
        for k in range(4):
            for dc in (0, 1):
                if k == 0 and dc == 0:
                    continue
                lanes = pl.ds(pl.multiple_of(((core + dc) % 2) * ROWS, 128), ROWS)
                for j, buf in enumerate((xe, xh)):
                    ref = buf.at[(z + 4 - k) % 4, :, lanes]
                    pltpu.make_async_remote_copy(
                        src_ref=ref,
                        dst_ref=ref,
                        send_sem=x_s.at[j, k * 2 + dc],
                        recv_sem=x_r.at[j, k * 2 + dc],
                        device_id=device(along(at, 2, k), (core + dc) % 2),
                        device_id_type=MESH,
                    ).wait_recv()

    for copy in x_copies():
        copy.start()

    h_gathers = [
        Gather(
            lambda s, r=r, n=n: gath.at[s + (pl.ds(r, n), slice(None))], order, h_s, h_r, 9 * p
        )
        for p, (order, (r, n)) in enumerate(zip(ORDERS, H_PARTS))
    ]
    for gather in h_gathers:
        gather.start(0)

    draft_gain = jnp.concatenate(
        [small[z, yy, zz, 2:3, :FEAT] for yy in range(4) for zz in range(4)], axis=1
    )
    token = turn(token_ref[...].astype(f32))
    base = (lax.axis_index("vocab") * VOC).astype(f32)

    for copy in own_copies:
        copy.wait()
    for k in (1, 3, 2):
        for j, dst in enumerate((we, wh)):
            ref = dst.at[(z + 4 - k) % 4]
            pltpu.make_async_remote_copy(
                src_ref=ref,
                dst_ref=ref,
                send_sem=w_s.at[j, k - 1],
                recv_sem=w_r.at[j, k - 1],
                device_id=device(along(at, 2, k), core),
                device_id_type=MESH,
            ).wait_recv()
    x_waits()

    def project(c, _):
        lanes = pl.ds(pl.multiple_of(c * ROWS, 128), ROWS)
        got = lax.dot_general(
            xe[:, :, lanes].reshape(4 * FEAT, ROWS), we[...].reshape(4 * FEAT, HALF), FIRST,
            preferred_element_type=f32,
        ) + lax.dot_general(
            xh[:, :, lanes].reshape(4 * FEAT, ROWS), wh[...].reshape(4 * FEAT, HALF), FIRST,
            preferred_element_type=f32,
        )
        part[:, c] = got.reshape(16, 16, HALF)
        return 0

    lax.fori_loop(0, 2, project, 0)

    def share(i):
        peer = (me32 + i) % 32
        return pltpu.make_async_remote_copy(
            src_ref=part.at[peer // 2, peer % 2],
            dst_ref=recv.at[me32],
            send_sem=rs_s.at[i],
            recv_sem=rs_r.at[i],
            device_id=device((peer // 8, (peer // 2) % 4, z), peer % 2),
            device_id_type=MESH,
        )

    def send_share(i, _):
        share(i).start()
        return 0

    lax.fori_loop(1, 32, send_share, 0)
    recv[me32] = part[me32 // 2, core]

    for gather in h_gathers:
        gather.wait(0)
        gather.start(1)
    for gather in h_gathers:
        gather.wait(1)
        gather.start(2)

    def wait_share(i, _):
        ref = recv.at[(me32 + 32 - i) % 32]
        peer = (me32 + i) % 32
        pltpu.make_async_remote_copy(
            src_ref=ref,
            dst_ref=ref,
            send_sem=rs_s.at[i],
            recv_sem=rs_r.at[i],
            device_id=device((peer // 8, (peer // 2) % 4, z), peer % 2),
            device_id_type=MESH,
        ).wait_recv()
        return 0

    lax.fori_loop(1, 32, wait_share, 0)

    def add(i, halves):
        return (halves[0] + recv[2 * i], halves[1] + recv[2 * i + 1])

    left, right = lax.fori_loop(1, 16, add, (recv[0], recv[1]))
    state = jnp.concatenate([left, right], axis=1)
    sq[z] = jnp.broadcast_to(jnp.sum(state * state, axis=1, keepdims=True), (16, 128))

    def q_copy(k, source):
        ref = sq.at[source]
        return pltpu.make_async_remote_copy(
            src_ref=ref,
            dst_ref=ref,
            send_sem=q_s.at[k - 1],
            recv_sem=q_r.at[k - 1],
            device_id=device(along(at, 2, k), core),
            device_id_type=MESH,
        )

    for k in (1, 3, 2):
        q_copy(k, z).start()
    for copy in head_copies:
        copy.wait()
    for k in (1, 3, 2):
        q_copy(k, (z + 4 - k) % 4).wait_recv()
    total = jnp.sum(sq[...], axis=0)[:, :1]
    gd[z, x, y] = (state * lax.rsqrt(total / D + epsilon) * draft_gain).astype(bf16)

    g_gathers = [
        Gather(
            lambda s, c=c, n=n: gd.at[s[2], s[0], s[1], :, pl.ds(c, n)], order, g_s, g_r, 9 * p
        )
        for p, (order, (c, n)) in enumerate(zip(ORDERS, G_PARTS))
    ]
    for gather in g_gathers:
        gather.start(0)

    for gather in h_gathers:
        gather.wait(2)

    def main_dot(q):
        got = lax.dot_general(
            gath[q].reshape(QUART, ROWS), head[pl.ds(q * QUART, QUART)], FIRST, preferred_element_type=f32
        )
        main_ref[...] = got if q == 0 else main_ref[...] + got

    main_dot(0)
    for gather in g_gathers:
        gather.wait(0)
        gather.start(1)
    main_dot(1)
    for gather in g_gathers:
        gather.wait(1)
        gather.start(2)
    main_dot(2)
    main_dot(3)

    def local_stats(ref):
        logits = ref[...]
        top = jnp.max(logits, axis=1, keepdims=True)
        return top, jnp.sum(jnp.exp(logits - top), axis=1, keepdims=True)

    main_top, main_sum = local_stats(main_ref)
    column = lax.broadcasted_iota(jnp.int32, (ROWS, VOC), 1).astype(f32) + base
    picked = jnp.sum(jnp.where(column == token[:, :1], main_ref[...], 0.0), axis=1, keepdims=True)

    for gather in g_gathers:
        gather.wait(2)

    def draft_dot(q):
        got = jnp.dot(
            gd[q].reshape(ROWS, QUART), head[pl.ds(q * QUART, QUART)], preferred_element_type=f32
        )
        draft_ref[...] = got if q == 0 else draft_ref[...] + got

    for q in range(4):
        draft_dot(q)
    draft_top, draft_sum = local_stats(draft_ref)

    lane = lax.broadcasted_iota(jnp.int32, (ROWS, 128), 1)
    packed = jnp.zeros((ROWS, 128), f32)
    for i, value in enumerate((main_top, main_sum, picked, draft_top, draft_sum)):
        packed = jnp.where(lane == i, value, packed)
    mine8 = packed.T[:8]

    def merge(tops, sums):
        top = jnp.max(tops, axis=0, keepdims=True)
        return top, jnp.sum(sums * jnp.exp(tops - top), axis=0, keepdims=True)

    for phase, axis in enumerate((2, 1, 0)):
        stats[phase, at[axis]] = mine8

        def st_copy(k, source):
            ref = stats.at[phase, source]
            return pltpu.make_async_remote_copy(
                src_ref=ref,
                dst_ref=ref,
                send_sem=st_s.at[phase * 3 + k - 1],
                recv_sem=st_r.at[phase * 3 + k - 1],
                device_id=device(along(at, axis, k), core),
                device_id_type=MESH,
            )

        for k in (1, 3, 2):
            st_copy(k, at[axis]).start()
        for k in (1, 3, 2):
            st_copy(k, (at[axis] + 4 - k) % 4).wait_recv()
        got = stats[phase]
        m_top, m_sum = merge(got[:, 0], got[:, 1])
        d_top, d_sum = merge(got[:, 3], got[:, 4])
        pick = jnp.sum(got[:, 2], axis=0, keepdims=True)
        mine8 = jnp.concatenate([m_top, m_sum, pick, d_top, d_sum, jnp.zeros((3, ROWS), f32)], axis=0)
        for k in (1, 3, 2):
            st_copy(k, at[axis]).wait_send()

    m_lse = m_top + jnp.log(m_sum)
    d_lse = d_top + jnp.log(d_sum)
    lse_ref[...] = jnp.concatenate([m_lse, d_lse, jnp.zeros((6, ROWS), f32)], axis=0)

    member = lax.broadcasted_iota(jnp.int32, (REQS, ROWS), 0) == request_ref[...]
    partial = jnp.sum(jnp.where(member, pick - m_lse, 0.0), axis=1, keepdims=True)
    score_buf[core] = jnp.broadcast_to(partial, (REQS, 128))

    def sc_copy(source):
        ref = score_buf.at[source]
        return pltpu.make_async_remote_copy(
            src_ref=ref,
            dst_ref=ref,
            send_sem=sc_s,
            recv_sem=sc_r,
            device_id=device(at, 1 - core),
            device_id_type=MESH,
        )

    sc_copy(core).start()

    small_gather.wait_sends()
    for k in (1, 3, 2):
        for copy in w_copies(k):
            copy.wait_send()
        q_copy(k, z).wait_send()
    for copy in x_copies():
        copy.wait_send()
    for gather in h_gathers + g_gathers:
        gather.wait_sends()

    def wait_sent(i, _):
        share(i).wait_send()
        return 0

    lax.fori_loop(1, 32, wait_sent, 0)
    sc_copy(1 - core).wait_recv()
    score_ref[...] = score_buf[0] + score_buf[1]
    sc_copy(core).wait_send()


def per_device(
    hidden,
    next_embedding,
    final_gain,
    hidden_gain,
    embed_gain,
    draft_gain,
    head_weight,
    proj_embed,
    proj_hidden,
    token_ids,
    row_request,
):
    gains = jnp.stack([final_gain, hidden_gain, embed_gain, draft_gain]).astype(f32)
    gains = jnp.pad(gains, ((0, 4), (0, 128 - FEAT)))
    vmem = pl.BlockSpec(memory_space=pltpu.VMEM)
    hbm = pl.BlockSpec(memory_space=pl.ANY)
    main, draft, lse, score = pl.pallas_call(
        kernel,
        name="heads",
        out_shape=(
            jax.ShapeDtypeStruct((ROWS, VOC), f32),
            jax.ShapeDtypeStruct((ROWS, VOC), f32),
            jax.ShapeDtypeStruct((8, ROWS), f32),
            jax.ShapeDtypeStruct((REQS, 128), f32),
        ),
        in_specs=[vmem] * 5 + [hbm] * 3,
        out_specs=(vmem,) * 4,
        scratch_shapes=[
            pltpu.VMEM((D, VOC), bf16),
            pltpu.VMEM((4, 4, 4, 8, ROWS), f32),
            pltpu.VMEM((4, 4, 4, FEAT, ROWS), bf16),
            pltpu.VMEM((4, FEAT, 2 * ROWS), bf16),
            pltpu.VMEM((4, FEAT, 2 * ROWS), bf16),
            pltpu.VMEM((4, FEAT, HALF), bf16),
            pltpu.VMEM((4, FEAT, HALF), bf16),
            pltpu.VMEM((16, 2, 16, HALF), f32),
            pltpu.VMEM((32, 16, HALF), f32),
            pltpu.VMEM((4, 16, 128), f32),
            pltpu.VMEM((4, 4, 4, 16, QUART), bf16),
            pltpu.VMEM((3, 4, 8, ROWS), f32),
            pltpu.VMEM((2, REQS, 128), f32),
            DMA((4,)),
            DMA((2,)),
            DMA((9,)),
            DMA((9,)),
            DMA((2, 3)),
            DMA((2, 3)),
            DMA((2, 8)),
            DMA((2, 8)),
            DMA((27,)),
            DMA((27,)),
            DMA((32,)),
            DMA((32,)),
            DMA((3,)),
            DMA((3,)),
            DMA((27,)),
            DMA((27,)),
            DMA((9,)),
            DMA((9,)),
            DMA,
            DMA,
        ],
        compiler_params=pltpu.CompilerParams(
            collective_id=0, has_side_effects=True, vmem_limit_bytes=48 * 2**20
        ),
        cost_estimate=pl.CostEstimate(flops=8_300_000_000, bytes_accessed=20_000_000, transcendentals=600_000),
    )(
        hidden.T,
        next_embedding.T,
        gains,
        token_ids[None, :],
        row_request[None, :],
        head_weight,
        proj_embed,
        proj_hidden,
    )
    return (main - lse[0][:, None], draft - lse[1][:, None], score[:, 0])


def solution(mesh):
    return jax.shard_map(
        per_device,
        mesh=mesh,
        in_specs=(
            P("req", "vocab"),
            P("req", "vocab"),
            P("vocab"),
            P("vocab"),
            P("vocab"),
            P("vocab"),
            P(None, "vocab"),
            P("vocab", None),
            P("vocab", None),
            P("req"),
            P("req"),
        ),
        out_specs=(P("req", "vocab"), P("req", "vocab"), P()),
        check_vma=False,
    )
```

```python
import jax
import jax.numpy as jnp
from jax import lax
from jax.experimental import pallas as pl
from jax.experimental.pallas import tpu as pltpu
from jax.sharding import PartitionSpec as P

D = 7168
REQS = 64
SIDE = 4
FEAT = 112
ROWS = 256
VOC = 1024
QUART = D // SIDE
HALF = QUART // 2

epsilon = 1e-06
MESH = pl.DeviceIdType.MESH
DMA = pltpu.SemaphoreType.DMA
f32 = jnp.float32
bf16 = jnp.bfloat16
FIRST = (((0,), (0,)), ((), ()))

H_ORDERS = ((2, 0, 1), (2, 1, 0), (0, 1, 2))
G_ORDERS = ((2, 1, 0), (0, 2, 1), (1, 0, 2))
H_PARTS = ((0, 80, 0, 128), (0, 80, 128, 128), (80, 32, 0, 256))
G_PARTS = ((0, 640), (640, 640), (1280, 512))

OTHERS = pl.ds(1, 3)
STEPS = {
    "0a": (0, (0, 0, 0)),
    "0b": (1, (0, 0, 0)),
    "0c": (2, (0, 0, 0)),
    "1b": (1, (OTHERS, 0, 0)),
    "1c": (2, (OTHERS, 0, 0)),
    "2c": (2, (0, OTHERS, 0)),
    "3c": (2, (OTHERS, OTHERS, 0)),
}


def coords():
    v = lax.axis_index("vocab")
    return (v // 16, (v // 4) % 4, v % 4)


def device(at, core):
    return (core, (at[0] * 4 + at[1]) * 4 + at[2])


def along(at, axis, step):
    moved = list(at)
    moved[axis] = (at[axis] + step) % 4
    return tuple(moved)


class Gather:
    def __init__(self, waits, name, view, order, send, recv, base):
        self.waits, self.name, self.view, self.order = waits, name, view, order
        self.sems, self.base = (send, recv), base

    def copy(self, step, k, landed):
        place, blocks = STEPS[step]
        there = list(blocks)
        there[place] = 4 - k
        index = self.base + list(STEPS).index(step) * 3 + k - 1
        src, dst = (self.view(tuple(b[self.order.index(a)] for a in range(3))) for b in (blocks, there))
        return pltpu.make_async_remote_copy(
            src_ref=dst if landed else src,
            dst_ref=dst,
            send_sem=self.sems[0].at[index],
            recv_sem=self.sems[1].at[index],
            device_id=device(along(coords(), self.order[place], k), lax.axis_index("req")),
            device_id_type=MESH,
        )

    def start(self, *steps):
        for step in steps:
            self.waits.send([self.copy(step, k, False) for k in (1, 3, 2)])

            def wait(step=step):
                for k in (1, 3, 2):
                    self.copy(step, k, True).wait_recv()

            self.waits.expect(self.name + step, wait)

    def wait(self, *steps):
        for step in steps:
            self.waits.receive(self.name + step)


def turn(row):
    return jnp.broadcast_to(row, (128, row.shape[1])).T


class Waits:
    def __init__(self):
        self.receives, self.sends = {}, []

    def send(self, copies):
        for copy in copies:
            copy.start()
        self.sends += copies

    def expect(self, name, wait):
        self.receives[name] = wait

    def receive(self, name):
        self.receives.pop(name)()

    def finish(self):
        for name in list(self.receives):
            self.receive(name)
        for copy in self.sends:
            copy.wait_send()


def kernel(
    hid_hbm, emb_hbm, gains_ref, token_hbm, request_hbm, head_ref, pe_ref, ph_ref,
    main_ref, draft_ref, lse_ref, score_ref,
    emb_ref, token_ref, request_ref,
    head, small, gath, normed, xe, xh, we, wh, part, got1, sum1, got2, sq, gd, acc, stats, score_buf,
    head_sem, own_sem,
    small_s, small_r, w_s, w_r, x_s, x_r, h_s, h_r, r1_s, r1_r, r2_s, r2_r, q_s, q_r, g_s, g_r,
    st_s, st_r, sc_s, sc_r,
):
    core = lax.axis_index("req")
    at = coords()
    x, y, z = at
    waits = Waits()

    def columns(zz):
        return pl.ds(pl.multiple_of(zz * QUART + core * HALF, 128), HALF)

    row_copies = [
        pltpu.make_async_copy(hid_hbm, gath.at[0, 0, 0], own_sem.at[2]),
        pltpu.make_async_copy(emb_hbm, emb_ref, own_sem.at[3]),
    ]
    id_copies = [
        pltpu.make_async_copy(token_hbm, token_ref, own_sem.at[4]),
        pltpu.make_async_copy(request_hbm, request_ref, own_sem.at[5]),
    ]
    own_copies = [
        pltpu.make_async_copy(pe_ref.at[:, columns(z)], we.at[z], own_sem.at[0]),
        pltpu.make_async_copy(ph_ref.at[:, columns(z)], wh.at[z], own_sem.at[1]),
    ]
    head_copies = [
        pltpu.make_async_copy(
            head_ref.at[pl.ds(i * QUART, QUART)], head.at[pl.ds(i * QUART, QUART)], head_sem.at[i]
        )
        for i in range(4)
    ]
    for copy in row_copies:
        copy.start()

    barrier = pltpu.get_barrier_semaphore()
    partners = [device(at, 1 - core)] + [
        device(along(at, axis, k), c) for axis in (2, 1, 0) for k in (1, 2, 3) for c in (0, 1)
    ]
    for partner in partners:
        pl.semaphore_signal(barrier, inc=1, device_id=partner, device_id_type=MESH)
    for copy in own_copies + id_copies + head_copies:
        copy.start()

    for copy in row_copies:
        copy.wait()
    hid = gath[0, 0, 0].astype(f32)
    emb = emb_ref[...].astype(f32)
    gains = gains_ref[...]

    def wide(row):
        return jnp.concatenate([row, row], axis=1)

    small[0, 0, 0] = jnp.concatenate(
        [
            jnp.sum(hid * hid, axis=0, keepdims=True),
            jnp.sum(emb * emb, axis=0, keepdims=True),
            wide(gains[3:4]),
            wide(gains[0:1]),
            jnp.zeros((4, ROWS), f32),
        ],
        axis=0,
    )
    pl.semaphore_wait(barrier, len(partners))

    def small_copy(phase, k, landed):
        blocks = [(0, 0, 0), (0, 0, pl.ds(0, 4)), (0, pl.ds(0, 4), pl.ds(0, 4))][phase]
        there = list(blocks)
        there[2 - phase] = 4 - k
        return pltpu.make_async_remote_copy(
            src_ref=small.at[tuple(there) if landed else blocks],
            dst_ref=small.at[tuple(there)],
            send_sem=small_s.at[phase * 3 + k - 1],
            recv_sem=small_r.at[phase * 3 + k - 1],
            device_id=device(along(at, 2 - phase, k), core),
            device_id_type=MESH,
        )

    def small_start(phase):
        waits.send([small_copy(phase, k, False) for k in (1, 3, 2)])

    def small_wait(phase):
        for k in (1, 3, 2):
            small_copy(phase, k, True).wait_recv()

    small_start(0)

    ha, hb, hc = [
        Gather(
            waits,
            "h%d" % p,
            lambda s, r=r, n=n, c=c, m=m: gath.at[s + (pl.ds(r, n), pl.ds(c, m))],
            order,
            h_s,
            h_r,
            21 * p,
        )
        for p, (order, (r, n, c, m)) in enumerate(zip(H_ORDERS, H_PARTS))
    ]
    ha.start("0a")
    hb.start("0a")
    hc.start("0a")

    w_pairs = ((pe_ref, we), (ph_ref, wh))

    def w_copy(k, j, src, dst):
        return pltpu.make_async_remote_copy(
            src_ref=src,
            dst_ref=dst,
            send_sem=w_s.at[j, k - 1],
            recv_sem=w_r.at[j, k - 1],
            device_id=device(along(at, 2, k), core),
            device_id_type=MESH,
        )

    for k in (1, 3, 2):
        waits.send([w_copy(k, j, src.at[:, columns((z + k) % 4)], dst.at[z]) for j, (src, dst) in enumerate(w_pairs)])

    def w_wait():
        for k in (1, 3, 2):
            for j, (_, dst) in enumerate(w_pairs):
                ref = dst.at[(z + 4 - k) % 4]
                w_copy(k, j, ref, ref).wait_recv()

    waits.expect("w", w_wait)

    small_wait(0)
    small_start(1)
    ha.start("0b", "0c")
    hb.start("0b", "0c")
    hc.start("0b")
    hidden_gain = turn(gains[1:2])[:FEAT, :1]
    embed_gain = turn(gains[2:3])[:FEAT, :1]
    small_wait(1)
    small_start(2)
    ha.wait("0a")
    hb.wait("0a")
    ha.start("1b")
    hb.start("1b")
    hc.wait("0a")
    hc.start("1b")
    small_wait(2)

    squares = jnp.sum(small[...].reshape(64, 8, ROWS), axis=0)
    hid_scale = lax.rsqrt(squares[0:1] / D + epsilon)
    emb_scale = lax.rsqrt(squares[1:2] / D + epsilon)
    mine = pl.ds(pl.multiple_of(core * ROWS, 128), ROWS)
    xe[z, :, mine] = (emb * emb_scale * embed_gain).astype(bf16)
    xh[z, :, mine] = (hid * hid_scale * hidden_gain).astype(bf16)

    line = [(k, dc) for k in range(4) for dc in (0, 1)][1:]

    def x_copy(k, dc, j, ref):
        return pltpu.make_async_remote_copy(
            src_ref=ref,
            dst_ref=ref,
            send_sem=x_s.at[j, k * 2 + dc],
            recv_sem=x_r.at[j, k * 2 + dc],
            device_id=device(along(at, 2, k), (core + dc) % 2),
            device_id_type=MESH,
        )

    for k, dc in line:
        waits.send([x_copy(k, dc, j, buf.at[z, :, mine]) for j, buf in enumerate((xe, xh))])

    def x_wait():
        for k, dc in line:
            lanes = pl.ds(pl.multiple_of(((core + dc) % 2) * ROWS, 128), ROWS)
            for j, buf in enumerate((xe, xh)):
                x_copy(k, dc, j, buf.at[(z + 4 - k) % 4, :, lanes]).wait_recv()

    waits.expect("x", x_wait)

    ha.start("1c")
    hb.start("1c")
    ha.wait("0b")
    hb.wait("0b")
    ha.start("2c")
    hb.start("2c")
    ha.wait("1b")
    ha.start("3c")
    hb.wait("1b")
    hb.start("3c")

    for copy in own_copies + id_copies:
        copy.wait()
    draft_gain = jnp.concatenate(
        [
            small[(z + 4 - x) % 4, (yy + 4 - y) % 4, (zz + 4 - z) % 4, 2:3, :FEAT]
            for yy in range(4)
            for zz in range(4)
        ],
        axis=1,
    )
    token = turn(token_ref[...].astype(f32))
    base = (lax.axis_index("vocab") * VOC).astype(f32)

    waits.receive("w")
    waits.receive("x")

    for c in (0, 1):
        lanes = pl.ds(c * ROWS, ROWS)
        rows = lax.dot_general(
            xe[:, :, lanes].reshape(4 * FEAT, ROWS), we[...].reshape(4 * FEAT, HALF), FIRST,
            preferred_element_type=f32,
        ) + lax.dot_general(
            xh[:, :, lanes].reshape(4 * FEAT, ROWS), wh[...].reshape(4 * FEAT, HALF), FIRST,
            preferred_element_type=f32,
        )
        part[:, :, c] = rows.reshape(4, 4, 2, 8, HALF)

    def r1_copy(half, k):
        to = (at[half] + k) % 4
        src = part.at[to, :, :, 0] if half == 0 else part.at[:, to, :, 1]
        return pltpu.make_async_remote_copy(
            src_ref=src,
            dst_ref=got1.at[half, k - 1],
            send_sem=r1_s.at[half * 3 + k - 1],
            recv_sem=r1_r.at[half * 3 + k - 1],
            device_id=device(along(at, half, k), core),
            device_id_type=MESH,
        )

    def r2_copy(half, k, dc):
        to = (core + dc) % 2
        axis = 1 - half
        return pltpu.make_async_remote_copy(
            src_ref=sum1.at[half, (at[axis] + k) % 4, to],
            dst_ref=got2.at[half, k * 2 + dc],
            send_sem=r2_s.at[half * 8 + k * 2 + dc],
            recv_sem=r2_r.at[half * 8 + k * 2 + dc],
            device_id=device(along(at, axis, k), to),
            device_id_type=MESH,
        )

    for k in (1, 3, 2):
        waits.send([r1_copy(0, k), r1_copy(1, k)])
    hc.wait("0b")
    hc.wait("1b")
    hc.start("0c", "1c", "2c", "3c")
    for half in (0, 1):
        own = part[x, :, :, 0] if half == 0 else part[:, y, :, 1]
        for k in (1, 3, 2):
            r1_copy(half, k).wait_recv()
            own = own + got1[half, k - 1]
        sum1[half] = own
        waits.send([r2_copy(half, k, dc) for k, dc in line])

    state_halves = []
    for half in (0, 1):
        for k, dc in line:
            r2_copy(half, k, dc).wait_recv()
        same = sum1[half, at[1 - half], core]
        for k in (1, 2, 3):
            same = same + got2[half, k * 2]
        other = got2[half, 1] + got2[half, 3] + got2[half, 5] + got2[half, 7]
        state_halves.append(
            jnp.concatenate(
                [jnp.where(core == 0, same, other), jnp.where(core == 0, other, same)], axis=1
            )
        )
    state = jnp.concatenate(state_halves, axis=0)
    sq[z] = jnp.broadcast_to(jnp.sum(state * state, axis=1, keepdims=True), (16, 128))

    def q_copy(k, source):
        ref = sq.at[source]
        return pltpu.make_async_remote_copy(
            src_ref=ref,
            dst_ref=ref,
            send_sem=q_s.at[k - 1],
            recv_sem=q_r.at[k - 1],
            device_id=device(along(at, 2, k), core),
            device_id_type=MESH,
        )

    waits.send([q_copy(k, z) for k in (1, 3, 2)])
    for copy in head_copies:
        copy.wait()
    for k in (1, 3, 2):
        q_copy(k, (z + 4 - k) % 4).wait_recv()
    total = jnp.sum(sq[...], axis=0)[:, :1]
    gd[0, 0, 0] = (state * lax.rsqrt(total / D + epsilon) * draft_gain).astype(bf16)

    gs = [
        Gather(waits, "g%d" % p, lambda s, c=c, n=n: gd.at[s + (slice(None), pl.ds(c, n))], order, g_s, g_r, 21 * p)
        for p, (order, (c, n)) in enumerate(zip(G_ORDERS, G_PARTS))
    ]
    for g in gs:
        g.start("0a")
    for g in gs:
        g.start("0b")
    for g in gs:
        g.start("0c")
    for g in gs:
        g.wait("0a")
        g.start("1b")
    for g in gs:
        g.wait("0b")
        g.start("1c", "2c")
    for h in (ha, hb):
        h.wait("0c", "1c", "2c", "3c")
    hc.wait("0c", "1c", "2c", "3c")

    def norm(xr, _):
        gain = small[xr].reshape(16, 8, ROWS)[:, 3, :128].T
        for yr in range(4):
            for zr in range(4):
                block = gath[xr, yr, zr].astype(f32) * hid_scale * gain[:FEAT, yr * 4 + zr : yr * 4 + zr + 1]
                normed[(x + xr) % 4, (y + yr) % 4, (z + zr) % 4] = block.astype(bf16)
        return 0

    lax.fori_loop(0, 4, norm, 0)
    for g in gs:
        g.wait("1b")
        g.start("3c")

    def main_dot(q):
        rows = lax.dot_general(
            normed[q].reshape(QUART, ROWS), head[pl.ds(q * QUART, QUART)], FIRST, preferred_element_type=f32
        )
        main_ref[...] = rows if q == 0 else main_ref[...] + rows

    for q in range(4):
        main_dot(q)

    def local_stats(ref):
        logits = ref[...]
        top = jnp.max(logits, axis=1, keepdims=True)
        return top, jnp.sum(jnp.exp(logits - top), axis=1, keepdims=True)

    main_top, main_sum = local_stats(main_ref)
    column = lax.broadcasted_iota(jnp.int32, (ROWS, VOC), 1).astype(f32) + base
    picked = jnp.sum(jnp.where(column == token[:, :1], main_ref[...], 0.0), axis=1, keepdims=True)

    for g in gs:
        g.wait("0c", "1c", "2c", "3c")

    for zr in range(4):
        there = pl.ds(pl.multiple_of(((z + zr) % 4) * QUART, 128), QUART)
        rows = jnp.dot(gd[:, :, zr].reshape(ROWS, QUART), head[there], preferred_element_type=f32)
        acc[...] = rows if zr == 0 else acc[...] + rows
    for xr in range(4):
        for yr in range(4):
            to = ((x + xr) % 4) * 4 + (y + yr) % 4
            draft_ref[pl.ds(pl.multiple_of(to * 16, 16), 16)] = acc[pl.ds((xr * 4 + yr) * 16, 16)]
    draft_top, draft_sum = local_stats(draft_ref)

    lane = lax.broadcasted_iota(jnp.int32, (ROWS, 128), 1)
    packed = jnp.zeros((ROWS, 128), f32)
    for i, value in enumerate((main_top, main_sum, picked, draft_top, draft_sum)):
        packed = jnp.where(lane == i, value, packed)
    mine8 = packed.T[:8]

    def merge(tops, sums):
        top = jnp.max(tops, axis=0, keepdims=True)
        return top, jnp.sum(sums * jnp.exp(tops - top), axis=0, keepdims=True)

    for phase, axis in enumerate((2, 1, 0)):
        stats[phase, at[axis]] = mine8

        def st_copy(k, source):
            ref = stats.at[phase, source]
            return pltpu.make_async_remote_copy(
                src_ref=ref,
                dst_ref=ref,
                send_sem=st_s.at[phase * 3 + k - 1],
                recv_sem=st_r.at[phase * 3 + k - 1],
                device_id=device(along(at, axis, k), core),
                device_id_type=MESH,
            )

        waits.send([st_copy(k, at[axis]) for k in (1, 3, 2)])
        for k in (1, 3, 2):
            st_copy(k, (at[axis] + 4 - k) % 4).wait_recv()
        got = stats[phase]
        m_top, m_sum = merge(got[:, 0], got[:, 1])
        d_top, d_sum = merge(got[:, 3], got[:, 4])
        pick = jnp.sum(got[:, 2], axis=0, keepdims=True)
        mine8 = jnp.concatenate([m_top, m_sum, pick, d_top, d_sum, jnp.zeros((3, ROWS), f32)], axis=0)

    m_lse = m_top + jnp.log(m_sum)
    d_lse = d_top + jnp.log(d_sum)
    lse_ref[...] = jnp.concatenate([m_lse, d_lse, jnp.zeros((6, ROWS), f32)], axis=0)

    member = lax.broadcasted_iota(jnp.int32, (REQS, ROWS), 0) == request_ref[...]
    partial = jnp.sum(jnp.where(member, pick - m_lse, 0.0), axis=1, keepdims=True)
    score_buf[core] = jnp.broadcast_to(partial, (REQS, 128))

    def sc_copy(source):
        ref = score_buf.at[source]
        return pltpu.make_async_remote_copy(
            src_ref=ref,
            dst_ref=ref,
            send_sem=sc_s,
            recv_sem=sc_r,
            device_id=device(at, 1 - core),
            device_id_type=MESH,
        )

    waits.send([sc_copy(core)])
    sc_copy(1 - core).wait_recv()
    score_ref[...] = score_buf[0] + score_buf[1]
    waits.finish()


def per_device(
    hidden,
    next_embedding,
    final_gain,
    hidden_gain,
    embed_gain,
    draft_gain,
    head_weight,
    proj_embed,
    proj_hidden,
    token_ids,
    row_request,
):
    gains = jnp.stack([final_gain, hidden_gain, embed_gain, draft_gain]).astype(f32)
    gains = jnp.pad(gains, ((0, 4), (0, 128 - FEAT)))
    vmem = pl.BlockSpec(memory_space=pltpu.VMEM)
    hbm = pl.BlockSpec(memory_space=pltpu.HBM)
    main, draft, lse, score = pl.pallas_call(
        kernel,
        name="heads",
        out_shape=(
            jax.ShapeDtypeStruct((ROWS, VOC), f32),
            jax.ShapeDtypeStruct((ROWS, VOC), f32),
            jax.ShapeDtypeStruct((8, ROWS), f32),
            jax.ShapeDtypeStruct((REQS, 128), f32),
        ),
        in_specs=[hbm] * 2 + [vmem] + [hbm] * 5,
        out_specs=(vmem,) * 4,
        scratch_shapes=[
            pltpu.VMEM((FEAT, ROWS), bf16),
            pltpu.VMEM((1, ROWS), jnp.int32),
            pltpu.VMEM((1, ROWS), jnp.int32),
            pltpu.VMEM((D, VOC), bf16),
            pltpu.VMEM((4, 4, 4, 8, ROWS), f32),
            pltpu.VMEM((4, 4, 4, FEAT, ROWS), bf16),
            pltpu.VMEM((4, 4, 4, FEAT, ROWS), bf16),
            pltpu.VMEM((4, FEAT, 2 * ROWS), bf16),
            pltpu.VMEM((4, FEAT, 2 * ROWS), bf16),
            pltpu.VMEM((4, FEAT, HALF), bf16),
            pltpu.VMEM((4, FEAT, HALF), bf16),
            pltpu.VMEM((4, 4, 2, 2, 8, HALF), f32),
            pltpu.VMEM((2, 3, 4, 2, 8, HALF), f32),
            pltpu.VMEM((2, 4, 2, 8, HALF), f32),
            pltpu.VMEM((2, 8, 8, HALF), f32),
            pltpu.VMEM((4, 16, 128), f32),
            pltpu.VMEM((4, 4, 4, 16, QUART), bf16),
            pltpu.VMEM((ROWS, VOC), f32),
            pltpu.VMEM((3, 4, 8, ROWS), f32),
            pltpu.VMEM((2, REQS, 128), f32),
            DMA((4,)),
            DMA((6,)),
            DMA((9,)),
            DMA((9,)),
            DMA((2, 3)),
            DMA((2, 3)),
            DMA((2, 8)),
            DMA((2, 8)),
            DMA((63,)),
            DMA((63,)),
            DMA((6,)),
            DMA((6,)),
            DMA((16,)),
            DMA((16,)),
            DMA((3,)),
            DMA((3,)),
            DMA((63,)),
            DMA((63,)),
            DMA((9,)),
            DMA((9,)),
            DMA,
            DMA,
        ],
        compiler_params=pltpu.CompilerParams(
            collective_id=0, has_side_effects=True, vmem_limit_bytes=58 * 2**20
        ),
        cost_estimate=pl.CostEstimate(flops=8_300_000_000, bytes_accessed=20_000_000, transcendentals=600_000),
    )(
        hidden.T,
        next_embedding.T,
        gains,
        token_ids[None, :],
        row_request[None, :],
        head_weight,
        proj_embed,
        proj_hidden,
    )
    return (main - lse[0][:, None], draft - lse[1][:, None], score[:, 0])


def solution(mesh):
    return jax.shard_map(
        per_device,
        mesh=mesh,
        in_specs=(
            P("req", "vocab"),
            P("req", "vocab"),
            P("vocab"),
            P("vocab"),
            P("vocab"),
            P("vocab"),
            P(None, "vocab"),
            P("vocab", None),
            P("vocab", None),
            P("req"),
            P("req"),
        ),
        out_specs=(P("req", "vocab"), P("req", "vocab"), P()),
        check_vma=False,
    )
```

```python
import jax
import jax.numpy as jnp
from jax import lax
from jax.experimental import pallas as pl
from jax.experimental.pallas import tpu as pltpu
from jax.sharding import PartitionSpec as P

D = 7168
REQS = 64
SIDE = 4
FEAT = 112
ROWS = 256
VOC = 1024
QUART = D // SIDE
HALF = QUART // 2

epsilon = 1e-06
MESH = pl.DeviceIdType.MESH
DMA = pltpu.SemaphoreType.DMA
f32 = jnp.float32
bf16 = jnp.bfloat16
FIRST = (((0,), (0,)), ((), ()))

H_ORDERS = ((2, 0, 1), (2, 1, 0), (0, 1, 2))
G_ORDERS = ((2, 1, 0), (0, 2, 1), (1, 0, 2))
H_EARLY = 64
H_PARTS = ((0, 64, 0, 128), (0, 64, 128, 128), (64, 48, 0, 256))
G_PARTS = ((0, 640), (640, 640), (1280, 512))

PIECES = ((0, 512), (512, 384))

OTHERS, ALL = pl.ds(1, 3), pl.ds(0, 4)
STEPS = {
    "0a": (0, (0, 0, 0)),
    "0b": (1, (0, 0, 0)),
    "1b": (1, (OTHERS, 0, 0)),
    "Lb": (1, (ALL, 0, 0)),
    "Lc": (2, (ALL, 0, 0)),
    "Pc": (2, (ALL, OTHERS, 0)),
    "Sc": (2, (ALL, ALL, 0)),
}


def coords():
    v = lax.axis_index("vocab")
    return (v // 16, (v // 4) % 4, v % 4)


def device(at, core):
    return (core, (at[0] * 4 + at[1]) * 4 + at[2])


def along(at, axis, step):
    moved = list(at)
    moved[axis] = (at[axis] + step) % 4
    return tuple(moved)


class Gather:
    def __init__(self, waits, name, view, order, send, recv, base):
        self.waits, self.name, self.view, self.order = waits, name, view, order
        self.sems, self.base = (send, recv), base

    def copy(self, step, k, landed):
        place, blocks = STEPS[step]
        there = list(blocks)
        there[place] = 4 - k
        index = self.base + list(STEPS).index(step) * 3 + k - 1
        src, dst = (self.view(tuple(b[self.order.index(a)] for a in range(3))) for b in (blocks, there))
        return pltpu.make_async_remote_copy(
            src_ref=dst if landed else src,
            dst_ref=dst,
            send_sem=self.sems[0].at[index],
            recv_sem=self.sems[1].at[index],
            device_id=device(along(coords(), self.order[place], k), lax.axis_index("req")),
            device_id_type=MESH,
        )

    def start(self, *steps):
        for step in steps:
            self.waits.send([self.copy(step, k, False) for k in (1, 3, 2)])

            def wait(step=step):
                for k in (1, 3, 2):
                    self.copy(step, k, True).wait_recv()

            self.waits.expect(self.name + step, wait)

    def wait(self, *steps):
        for step in steps:
            self.waits.receive(self.name + step)


def turn(row):
    return jnp.broadcast_to(row, (128, row.shape[1])).T


class Waits:
    def __init__(self):
        self.receives, self.sends = {}, []

    def send(self, copies):
        for copy in copies:
            copy.start()
        self.sends += copies

    def expect(self, name, wait):
        self.receives[name] = wait

    def receive(self, name):
        self.receives.pop(name)()

    def finish(self):
        for name in list(self.receives):
            self.receive(name)
        for copy in self.sends:
            copy.wait_send()


def kernel(
    hid_hbm, emb_hbm, rows_ref, token_hbm, request_hbm, head_ref, pe_ref, ph_ref,
    main_hbm, draft_hbm, main_lse_ref, draft_lse_ref, score_ref,
    main_ref, draft_ref, token_ref, request_ref, head, small, gath, normed, xraw, xsq, xe, xh, we, wh, part, got1, sum1, got2, sq, gd, acc, stats, score_buf,
    head_sem, own_sem,
    small_s, small_r, w_s, w_r, x_s, x_r, h_s, h_r, r1_s, r1_r, r2_s, r2_r, q_s, q_r, g_s, g_r,
    st_s, st_r, sc_s, sc_r,
):
    core = lax.axis_index("req")
    at = coords()
    x, y, z = at
    waits = Waits()
    mine = pl.ds(pl.multiple_of(core * ROWS, 128), ROWS)

    def columns(zz):
        return pl.ds(pl.multiple_of(zz * QUART + core * HALF, 128), HALF)

    row_copies = [
        pltpu.make_async_copy(hid_hbm, xraw.at[z, 1, :, mine], own_sem.at[2]),
        pltpu.make_async_copy(emb_hbm, xraw.at[z, 0, :, mine], own_sem.at[3]),
        pltpu.make_async_copy(hid_hbm, gath.at[0, 0, 0], own_sem.at[4]),
    ]
    own_copies = [
        pltpu.make_async_copy(token_hbm, token_ref, own_sem.at[5]),
        pltpu.make_async_copy(request_hbm, request_ref, own_sem.at[6]),
        pltpu.make_async_copy(pe_ref.at[:, columns(z)], we.at[z], own_sem.at[0]),
        pltpu.make_async_copy(ph_ref.at[:, columns(z)], wh.at[z], own_sem.at[1]),
    ]
    head_copies = [
        pltpu.make_async_copy(
            head_ref.at[pl.ds(i * QUART, QUART)], head.at[pl.ds(i * QUART, QUART)], head_sem.at[i]
        )
        for i in range(4)
    ]
    for copy in row_copies:
        copy.start()

    barrier = pltpu.get_barrier_semaphore()
    partners = [device(at, 1 - core)] + [
        device(along(at, axis, k), c) for axis in (2, 1, 0) for k in (1, 2, 3) for c in (0, 1)
    ]
    for partner in partners:
        pl.semaphore_signal(barrier, inc=1, device_id=partner, device_id_type=MESH)
    for copy in own_copies + head_copies:
        copy.start()

    for copy in row_copies:
        copy.wait()
    emb = xraw[z, 0, :, mine].astype(f32)
    hid = xraw[z, 1, :, mine].astype(f32)
    small[0, 0, 0] = jnp.concatenate(
        [
            jnp.sum(emb * emb, axis=0, keepdims=True),
            jnp.sum(hid * hid, axis=0, keepdims=True),
            rows_ref[0:4],
            jnp.zeros((2, ROWS), f32),
        ],
        axis=0,
    )
    pl.semaphore_wait(barrier, len(partners))

    def small_copy(phase, k, landed):
        blocks = [(0, 0, 0), (0, 0, pl.ds(0, 4)), (0, pl.ds(0, 4), pl.ds(0, 4))][phase]
        there = list(blocks)
        there[2 - phase] = 4 - k
        return pltpu.make_async_remote_copy(
            src_ref=small.at[tuple(there) if landed else blocks],
            dst_ref=small.at[tuple(there)],
            send_sem=small_s.at[phase * 3 + k - 1],
            recv_sem=small_r.at[phase * 3 + k - 1],
            device_id=device(along(at, 2 - phase, k), core),
            device_id_type=MESH,
        )

    def small_start(phase):
        waits.send([small_copy(phase, k, False) for k in (1, 3, 2)])

    def small_wait(phase):
        for k in (1, 3, 2):
            small_copy(phase, k, True).wait_recv()

    def x_copy(k, forward):
        to = ((core + 1) % 2) if forward or k == 0 else core
        ref = xraw.at[(z + 4 - k) % 4 if forward else z, :, :, mine]
        index = k + 3 if forward else k
        return pltpu.make_async_remote_copy(
            src_ref=ref,
            dst_ref=ref,
            send_sem=x_s.at[index],
            recv_sem=x_r.at[index],
            device_id=device(at if forward else along(at, 2, k), to),
            device_id_type=MESH,
        )

    def x_wait(k, forward):
        other = pl.ds(pl.multiple_of((1 - core) * ROWS, 128), ROWS)
        ref = xraw.at[(z + 4 - k) % 4, :, :, other if forward or k == 0 else mine]
        index = k + 3 if forward else k
        pltpu.make_async_remote_copy(
            src_ref=ref,
            dst_ref=ref,
            send_sem=x_s.at[index],
            recv_sem=x_r.at[index],
            device_id=device(at, 1 - core),
            device_id_type=MESH,
        ).wait_recv()

    def x_arrive():
        for k in (1, 3, 2):
            x_wait(k, False)
            waits.send([x_copy(k, True)])

    def x_all():
        for k in (1, 3, 2):
            x_wait(k, True)
        x_wait(0, False)

    small_start(0)
    waits.send([x_copy(k, False) for k in (1, 3, 2, 0)])
    waits.expect("x", x_arrive)
    waits.expect("x forwarded", x_all)

    ha, hb, hc = [
        Gather(
            waits,
            "h%d" % p,
            lambda s, r=r, n=n, c=c, m=m: gath.at[s + (pl.ds(r, n), pl.ds(c, m))],
            order,
            h_s,
            h_r,
            21 * p,
        )
        for p, (order, (r, n, c, m)) in enumerate(zip(H_ORDERS, H_PARTS))
    ]
    w_pairs = ((pe_ref, we), (ph_ref, wh))

    def w_copy(k, j, p, src, dst):
        return pltpu.make_async_remote_copy(
            src_ref=src,
            dst_ref=dst,
            send_sem=w_s.at[j, p * 3 + k - 1],
            recv_sem=w_r.at[j, p * 3 + k - 1],
            device_id=device(along(at, 2, k), core),
            device_id_type=MESH,
        )

    def w_start(p):
        c, n = PIECES[p]
        for k in (1, 3, 2):
            there = pl.ds(pl.multiple_of((z + k) % 4 * QUART + core * HALF + c, 128), n)
            waits.send(
                [
                    w_copy(k, j, p, src.at[:, there], dst.at[z, :, pl.ds(c, n)])
                    for j, (src, dst) in enumerate(w_pairs)
                ]
            )

        def w_wait(ks):
            for k in ks:
                for j, (_, dst) in enumerate(w_pairs):
                    ref = dst.at[(z + 4 - k) % 4, :, pl.ds(c, n)]
                    w_copy(k, j, p, ref, ref).wait_recv()

        waits.expect("w%dnear" % p, lambda: w_wait((1, 3)))
        waits.expect("w%d" % p, lambda: w_wait((2,)))

    small_wait(0)
    small_start(1)
    hc.start("0a", "0b")
    waits.receive("x")
    w_start(0)
    w_start(1)
    small_wait(1)
    small_start(2)
    for zr in (1, 2, 3):
        gath[0, 0, zr, :H_EARLY] = xraw[(z + zr) % 4, 1, :H_EARLY, mine]
    ha.start("Lb")
    hb.start("Lb")
    hc.wait("0a")
    hc.start("1b")
    ha.start("Lc")
    hb.start("Lc")
    small_wait(2)

    xsq[core] = jnp.sum(small[...].reshape(64, 8, ROWS), axis=0)

    def xsq_copy(which):
        ref = xsq.at[which]
        return pltpu.make_async_remote_copy(
            src_ref=ref,
            dst_ref=ref,
            send_sem=x_s.at[7],
            recv_sem=x_r.at[7],
            device_id=device(at, 1 - core),
            device_id_type=MESH,
        )

    waits.send([xsq_copy(core)])
    waits.expect("xsq", xsq_copy(1 - core).wait_recv)

    ha.wait("Lb")
    ha.start("Pc")
    hb.wait("Lb")
    hb.start("Pc")

    waits.receive("x forwarded")
    waits.receive("xsq")
    hid_scale = lax.rsqrt(xsq[core, 1:2] / D + epsilon)
    scales = [
        lax.rsqrt(jnp.concatenate([xsq[0, j : j + 1], xsq[1, j : j + 1]], axis=1) / D + epsilon) for j in (0, 1)
    ]
    for zr in range(4):
        block_gains = small[0, 0, zr, :, :128].T
        there = (z + zr) % 4
        for j, buf in enumerate((xe, xh)):
            raw = xraw[there, j].astype(f32)
            buf[there] = (raw * scales[j] * block_gains[:FEAT, 5 - j : 6 - j]).astype(bf16)
    for copy in own_copies:
        copy.wait()
    draft_gain = jnp.concatenate(
        [
            small[(z + 4 - x) % 4, (yy + 4 - y) % 4, (zz + 4 - z) % 4, 2:3, :FEAT]
            for yy in range(4)
            for zz in range(4)
        ],
        axis=1,
    )
    token = turn(token_ref[...].astype(f32))
    base = (lax.axis_index("vocab") * VOC).astype(f32)

    line = [(k, dc) for k in range(4) for dc in (0, 1)][1:]

    def r1_copy(p, half, k):
        lanes = pl.ds(*PIECES[p])
        to = (at[half] + k) % 4
        src = part.at[to, :, :, 0, :, lanes] if half == 0 else part.at[:, to, :, 1, :, lanes]
        return pltpu.make_async_remote_copy(
            src_ref=src,
            dst_ref=got1.at[half, k - 1, :, :, :, lanes],
            send_sem=r1_s.at[p * 6 + half * 3 + k - 1],
            recv_sem=r1_r.at[p * 6 + half * 3 + k - 1],
            device_id=device(along(at, half, k), core),
            device_id_type=MESH,
        )

    def r2_copy(p, half, k, dc):
        lanes = pl.ds(*PIECES[p])
        to = (core + dc) % 2
        axis = 1 - half
        return pltpu.make_async_remote_copy(
            src_ref=sum1.at[half, (at[axis] + k) % 4, to, :, lanes],
            dst_ref=got2.at[half, k * 2 + dc, :, lanes],
            send_sem=r2_s.at[p * 16 + half * 8 + k * 2 + dc],
            recv_sem=r2_r.at[p * 16 + half * 8 + k * 2 + dc],
            device_id=device(along(at, axis, k), to),
            device_id_type=MESH,
        )

    for p, (c0, n) in enumerate(PIECES):
        lanes = pl.ds(c0, n)
        waits.receive("w%dnear" % p)
        waits.receive("w%d" % p)
        for c in (0, 1):
            reqs = pl.ds(c * ROWS, ROWS)
            rows = lax.dot_general(
                xe[:, :, reqs].reshape(4 * FEAT, ROWS), we[:, :, lanes].reshape(4 * FEAT, n), FIRST,
                preferred_element_type=f32,
            ) + lax.dot_general(
                xh[:, :, reqs].reshape(4 * FEAT, ROWS), wh[:, :, lanes].reshape(4 * FEAT, n), FIRST,
                preferred_element_type=f32,
            )
            part[:, :, c, :, :, lanes] = rows.reshape(4, 4, 2, 8, n)
        for half in (0, 1):
            for k in (1, 3, 2):
                waits.send([r1_copy(p, half, k)])
                waits.expect("r1%d%d%d" % (p, half, k), r1_copy(p, half, k).wait_recv)
    hc.wait("0b", "1b")
    hc.start("Sc")
    for p, (c0, n) in enumerate(PIECES):
        lanes = pl.ds(c0, n)
        for half in (0, 1):
            own = part[x, :, :, 0, :, lanes] if half == 0 else part[:, y, :, 1, :, lanes]
            for k in (1, 3, 2):
                waits.receive("r1%d%d%d" % (p, half, k))
                own = own + got1[half, k - 1, :, :, :, lanes]
            sum1[half, :, :, :, lanes] = own
            for k, dc in line:
                waits.send([r2_copy(p, half, k, dc)])
                waits.expect("r2%d%d%d%d" % (p, half, k, dc), r2_copy(p, half, k, dc).wait_recv)

    state_halves = []
    for half in (0, 1):
        for p in (0, 1):
            for k, dc in line:
                waits.receive("r2%d%d%d%d" % (p, half, k, dc))
        same = sum1[half, at[1 - half], core]
        for k in (1, 2, 3):
            same = same + got2[half, k * 2]
        other = got2[half, 1] + got2[half, 3] + got2[half, 5] + got2[half, 7]
        state_halves.append(
            jnp.concatenate(
                [jnp.where(core == 0, same, other), jnp.where(core == 0, other, same)], axis=1
            )
        )
    state = jnp.concatenate(state_halves, axis=0)
    sq[z] = jnp.broadcast_to(jnp.sum(state * state, axis=1, keepdims=True), (16, 128))

    def q_copy(k, source):
        ref = sq.at[source]
        return pltpu.make_async_remote_copy(
            src_ref=ref,
            dst_ref=ref,
            send_sem=q_s.at[k - 1],
            recv_sem=q_r.at[k - 1],
            device_id=device(along(at, 2, k), core),
            device_id_type=MESH,
        )

    waits.send([q_copy(k, z) for k in (1, 3, 2)])
    for k in (1, 3, 2):
        waits.expect("q%d" % k, q_copy(k, (z + 4 - k) % 4).wait_recv)
    ha.wait("Lc", "Pc")
    hb.wait("Lc", "Pc")
    hc.wait("Sc")

    def norm(xr, _):
        gain = small[xr].reshape(16, 8, ROWS)[:, 3, :128].T
        for yr in range(4):
            for zr in range(4):
                block = gath[xr, yr, zr].astype(f32) * hid_scale * gain[:FEAT, yr * 4 + zr : yr * 4 + zr + 1]
                normed[(x + xr) % 4, (y + yr) % 4, (z + zr) % 4] = block.astype(bf16)
        return 0

    lax.fori_loop(0, 4, norm, 0)
    for copy in head_copies:
        copy.wait()
    for k in (1, 3, 2):
        waits.receive("q%d" % k)
    total = jnp.sum(sq[...], axis=0)[:, :1]
    gd[0, 0, 0] = (state * lax.rsqrt(total / D + epsilon) * draft_gain).astype(bf16)

    earlier = list(waits.sends)
    gs = [
        Gather(waits, "g%d" % p, lambda s, c=c, n=n: gd.at[s + (slice(None), pl.ds(c, n))], order, g_s, g_r, 21 * p)
        for p, (order, (c, n)) in enumerate(zip(G_ORDERS, G_PARTS))
    ]
    for g in gs:
        g.start("0a")
    def main_dot(q):
        rows = lax.dot_general(
            normed[q].reshape(QUART, ROWS), head[pl.ds(q * QUART, QUART)], FIRST, preferred_element_type=f32
        )
        main_ref[...] = rows if q == 0 else main_ref[...] + rows

    for g in gs:
        g.wait("0a")
        g.start("Lb")
    for g in gs:
        g.start("Lc")
    main_dot(0)
    for g in gs:
        g.wait("Lb")
        g.start("Pc")
    main_dot(1)
    main_dot(2)
    main_dot(3)

    def local_stats(ref):
        logits = ref[...]
        top = jnp.max(logits, axis=1, keepdims=True)
        return top, jnp.sum(jnp.exp(logits - top), axis=1, keepdims=True)

    main_out = pltpu.make_async_copy(main_ref, main_hbm, own_sem.at[7])
    main_out.start()
    main_top, main_sum = local_stats(main_ref)
    column = lax.broadcasted_iota(jnp.int32, (ROWS, VOC), 1).astype(f32) + base
    picked = jnp.sum(jnp.where(column == token[:, :1], main_ref[...], 0.0), axis=1, keepdims=True)

    def pack(values):
        lane = lax.broadcasted_iota(jnp.int32, (ROWS, 128), 1)
        packed = jnp.zeros((ROWS, 128), f32)
        for i, value in enumerate(values):
            packed = jnp.where(lane == i, value, packed)
        return packed.T[:8]

    def st_copy(which, phase, k, source):
        ref = stats.at[which, phase, source]
        index = which * 9 + phase * 3 + k - 1
        return pltpu.make_async_remote_copy(
            src_ref=ref,
            dst_ref=ref,
            send_sem=st_s.at[index],
            recv_sem=st_r.at[index],
            device_id=device(along(at, 2 - phase, k), core),
            device_id_type=MESH,
        )

    def st_start(which, phase, block):
        here = at[2 - phase]
        stats[which, phase, here] = block
        waits.send([st_copy(which, phase, k, here) for k in (1, 3, 2)])
        for k in (1, 3, 2):
            source = (here + 4 - k) % 4
            waits.expect("st%d%d%d" % (which, phase, k), st_copy(which, phase, k, source).wait_recv)

    def st_finish(which, phase):
        for k in (1, 3, 2):
            waits.receive("st%d%d%d" % (which, phase, k))
        got = stats[which, phase]
        tops = got[:, 0]
        top = jnp.max(tops, axis=0, keepdims=True)
        total = jnp.sum(got[:, 1] * jnp.exp(tops - top), axis=0, keepdims=True)
        pick = jnp.sum(got[:, 2], axis=0, keepdims=True)
        return jnp.concatenate([top, total, pick, jnp.zeros((5, ROWS), f32)], axis=0)

    st_start(0, 0, pack((main_top, main_sum, picked)))
    for copy in earlier:
        copy.wait_send()
    waits.sends = waits.sends[len(earlier) :]

    for g in gs:
        g.wait("Lc", "Pc")

    def draft_dot(zr):
        there = pl.ds(pl.multiple_of(((z + zr) % 4) * QUART, 128), QUART)
        rows = jnp.dot(gd[:, :, zr].reshape(ROWS, QUART), head[there], preferred_element_type=f32)
        acc[...] = rows if zr == 0 else acc[...] + rows

    draft_dot(0)
    draft_dot(1)
    st_start(0, 1, st_finish(0, 0))
    draft_dot(2)
    draft_dot(3)
    for xr in range(4):
        for yr in range(4):
            to = ((x + xr) % 4) * 4 + (y + yr) % 4
            draft_ref[pl.ds(pl.multiple_of(to * 16, 16), 16)] = acc[pl.ds((xr * 4 + yr) * 16, 16)]
    draft_out = pltpu.make_async_copy(draft_ref, draft_hbm, own_sem.at[8])
    draft_out.start()
    draft_top, draft_sum = local_stats(draft_ref)
    st_start(1, 0, pack((draft_top, draft_sum)))
    st_start(0, 2, st_finish(0, 1))
    st_start(1, 1, st_finish(1, 0))
    main_all = st_finish(0, 2)
    main_lse = main_all[0:1] + jnp.log(main_all[1:2])
    main_lse_ref[...] = main_lse

    member = lax.broadcasted_iota(jnp.int32, (REQS, ROWS), 0) == request_ref[...]
    partial = jnp.sum(jnp.where(member, main_all[2:3] - main_lse, 0.0), axis=1, keepdims=True)
    score_buf[core] = jnp.broadcast_to(partial, (REQS, 128))

    def sc_copy(source):
        ref = score_buf.at[source]
        return pltpu.make_async_remote_copy(
            src_ref=ref,
            dst_ref=ref,
            send_sem=sc_s,
            recv_sem=sc_r,
            device_id=device(at, 1 - core),
            device_id_type=MESH,
        )

    waits.send([sc_copy(core)])
    st_start(1, 2, st_finish(1, 1))
    sc_copy(1 - core).wait_recv()
    score_ref[...] = (score_buf[0] + score_buf[1]).T[:1]
    draft_all = st_finish(1, 2)
    draft_lse_ref[...] = draft_all[0:1] + jnp.log(draft_all[1:2])
    main_out.wait()
    draft_out.wait()
    waits.finish()


def per_device(
    hidden,
    next_embedding,
    final_gain,
    hidden_gain,
    embed_gain,
    draft_gain,
    head_weight,
    proj_embed,
    proj_hidden,
    token_ids,
    row_request,
):
    rows = jnp.stack([draft_gain, final_gain, hidden_gain, embed_gain]).astype(f32)
    rows = jnp.pad(rows, ((0, 4), (0, ROWS - FEAT)))
    vmem = pl.BlockSpec(memory_space=pltpu.VMEM)
    hbm = pl.BlockSpec(memory_space=pltpu.HBM)
    main, draft, main_lse, draft_lse, score = pl.pallas_call(
        kernel,
        name="heads",
        out_shape=(
            jax.ShapeDtypeStruct((ROWS, VOC), f32),
            jax.ShapeDtypeStruct((ROWS, VOC), f32),
            jax.ShapeDtypeStruct((1, ROWS), f32),
            jax.ShapeDtypeStruct((1, ROWS), f32),
            jax.ShapeDtypeStruct((1, REQS), f32),
        ),
        in_specs=[hbm] * 2 + [vmem] + [hbm] * 5,
        out_specs=(hbm,) * 2 + (vmem,) * 3,
        scratch_shapes=[
            pltpu.VMEM((ROWS, VOC), f32),
            pltpu.VMEM((ROWS, VOC), f32),
            pltpu.VMEM((1, ROWS), jnp.int32),
            pltpu.VMEM((1, ROWS), jnp.int32),
            pltpu.VMEM((D, VOC), bf16),
            pltpu.VMEM((4, 4, 4, 8, ROWS), f32),
            pltpu.VMEM((4, 4, 4, FEAT, ROWS), bf16),
            pltpu.VMEM((4, 4, 4, FEAT, ROWS), bf16),
            pltpu.VMEM((4, 2, FEAT, 2 * ROWS), bf16),
            pltpu.VMEM((2, 8, ROWS), f32),
            pltpu.VMEM((4, FEAT, 2 * ROWS), bf16),
            pltpu.VMEM((4, FEAT, 2 * ROWS), bf16),
            pltpu.VMEM((4, FEAT, HALF), bf16),
            pltpu.VMEM((4, FEAT, HALF), bf16),
            pltpu.VMEM((4, 4, 2, 2, 8, HALF), f32),
            pltpu.VMEM((2, 3, 4, 2, 8, HALF), f32),
            pltpu.VMEM((2, 4, 2, 8, HALF), f32),
            pltpu.VMEM((2, 8, 8, HALF), f32),
            pltpu.VMEM((4, 16, 128), f32),
            pltpu.VMEM((4, 4, 4, 16, QUART), bf16),
            pltpu.VMEM((ROWS, VOC), f32),
            pltpu.VMEM((2, 3, 4, 8, ROWS), f32),
            pltpu.VMEM((2, REQS, 128), f32),
            DMA((4,)),
            DMA((9,)),
            DMA((9,)),
            DMA((9,)),
            DMA((2, 6)),
            DMA((2, 6)),
            DMA((8,)),
            DMA((8,)),
            DMA((63,)),
            DMA((63,)),
            DMA((12,)),
            DMA((12,)),
            DMA((32,)),
            DMA((32,)),
            DMA((3,)),
            DMA((3,)),
            DMA((63,)),
            DMA((63,)),
            DMA((18,)),
            DMA((18,)),
            DMA,
            DMA,
        ],
        compiler_params=pltpu.CompilerParams(
            collective_id=0, has_side_effects=True, vmem_limit_bytes=58 * 2**20
        ),
        cost_estimate=pl.CostEstimate(flops=8_300_000_000, bytes_accessed=20_000_000, transcendentals=600_000),
    )(
        hidden.T,
        next_embedding.T,
        rows,
        token_ids[None, :],
        row_request[None, :],
        head_weight,
        proj_embed,
        proj_hidden,
    )
    return (main - main_lse[0][:, None], draft - draft_lse[0][:, None], score[0])


def solution(mesh):
    return jax.shard_map(
        per_device,
        mesh=mesh,
        in_specs=(
            P("req", "vocab"),
            P("req", "vocab"),
            P("vocab"),
            P("vocab"),
            P("vocab"),
            P("vocab"),
            P(None, "vocab"),
            P("vocab", None),
            P("vocab", None),
            P("req"),
            P("req"),
        ),
        out_specs=(P("req", "vocab"), P("req", "vocab"), P()),
        check_vma=False,
    )
```

```python
import jax
import jax.numpy as jnp
from jax import lax
from jax.experimental import pallas as pl
from jax.experimental.pallas import tpu as pltpu
from jax.sharding import PartitionSpec as P

D = 7168
REQS = 64
SIDE = 4
FEAT = 112
ROWS = 256
VOC = 1024
QUART = D // SIDE
HALF = QUART // 2

epsilon = 1e-06
MESH = pl.DeviceIdType.MESH
DMA = pltpu.SemaphoreType.DMA
f32 = jnp.float32
bf16 = jnp.bfloat16
FIRST = (((0,), (0,)), ((), ()))

H_ORDERS = ((2, 0, 1), (2, 1, 0), (0, 1, 2))
G_ORDERS = ((2, 1, 0), (0, 2, 1), (1, 0, 2))
H_EARLY = 64
H_PARTS = ((0, 64, 0, 128), (0, 64, 128, 128), (64, 48, 0, 256))
G_PARTS = ((0, 640), (640, 640), (1280, 512))

PIECES = ((0, 512), (512, 384))

OTHERS, ALL = pl.ds(1, 3), pl.ds(0, 4)
STEPS = {
    "0a": (0, (0, 0, 0)),
    "0b": (1, (0, 0, 0)),
    "1b": (1, (OTHERS, 0, 0)),
    "Lb": (1, (ALL, 0, 0)),
    "Lc": (2, (ALL, 0, 0)),
    "Pc": (2, (ALL, OTHERS, 0)),
    "Sc": (2, (ALL, ALL, 0)),
}


def coords():
    v = lax.axis_index("vocab")
    return (v // 16, (v // 4) % 4, v % 4)


def device(at, core):
    return (core, (at[0] * 4 + at[1]) * 4 + at[2])


def along(at, axis, step):
    moved = list(at)
    moved[axis] = (at[axis] + step) % 4
    return tuple(moved)


class Gather:
    def __init__(self, waits, name, view, order, send, recv, base):
        self.waits, self.name, self.view, self.order = waits, name, view, order
        self.sems, self.base = (send, recv), base

    def copy(self, step, k, landed):
        place, blocks = STEPS[step]
        there = list(blocks)
        there[place] = 4 - k
        index = self.base + list(STEPS).index(step) * 3 + k - 1
        src, dst = (self.view(tuple(b[self.order.index(a)] for a in range(3))) for b in (blocks, there))
        return pltpu.make_async_remote_copy(
            src_ref=dst if landed else src,
            dst_ref=dst,
            send_sem=self.sems[0].at[index],
            recv_sem=self.sems[1].at[index],
            device_id=device(along(coords(), self.order[place], k), lax.axis_index("req")),
            device_id_type=MESH,
        )

    def start(self, *steps):
        for step in steps:
            self.waits.send([self.copy(step, k, False) for k in (1, 3, 2)])

            def wait(step=step):
                for k in (1, 3, 2):
                    self.copy(step, k, True).wait_recv()

            self.waits.expect(self.name + step, wait)

    def wait(self, *steps):
        for step in steps:
            self.waits.receive(self.name + step)


def turn(row):
    return jnp.broadcast_to(row, (128, row.shape[1])).T


class Waits:
    def __init__(self):
        self.receives, self.sends = {}, []

    def send(self, copies):
        for copy in copies:
            copy.start()
        self.sends += copies

    def expect(self, name, wait):
        self.receives[name] = wait

    def receive(self, name):
        self.receives.pop(name)()

    def finish(self):
        for name in list(self.receives):
            self.receive(name)
        for copy in self.sends:
            copy.wait_send()


def kernel(
    hid_hbm, emb_hbm, gain_a, gain_b, gain_c, gain_d, token_hbm, request_hbm, head_ref, pe_ref, ph_ref,
    main_hbm, draft_hbm, main_lse_ref, draft_lse_ref, score_ref,
    main_ref, draft_ref, near_a, near_b, near_c, near_d, token_ref, request_ref, head, small, gath, normed, xraw, xsq, xe, xh, we, wh, part, got1, sum1, got2, sq, gd, acc, stats, score_buf,
    head_sem, own_sem,
    small_s, small_r, w_s, w_r, x_s, x_r, h_s, h_r, r1_s, r1_r, r2_s, r2_r, q_s, q_r, g_s, g_r,
    st_s, st_r, sc_s, sc_r,
):
    core = lax.axis_index("req")
    at = coords()
    x, y, z = at
    waits = Waits()
    mine = pl.ds(pl.multiple_of(core * ROWS, 128), ROWS)

    def columns(zz):
        return pl.ds(pl.multiple_of(zz * QUART + core * HALF, 128), HALF)

    row_copies = [
        pltpu.make_async_copy(hid_hbm, xraw.at[z, 1, :, mine], own_sem.at[2]),
        pltpu.make_async_copy(emb_hbm, xraw.at[z, 0, :, mine], own_sem.at[3]),
        pltpu.make_async_copy(hid_hbm, gath.at[0, 0, 0], own_sem.at[4]),
    ]
    own_copies = [
        pltpu.make_async_copy(token_hbm, token_ref, own_sem.at[5]),
        pltpu.make_async_copy(request_hbm, request_ref, own_sem.at[6]),
        pltpu.make_async_copy(pe_ref.at[:, columns(z)], we.at[z], own_sem.at[0]),
        pltpu.make_async_copy(ph_ref.at[:, columns(z)], wh.at[z], own_sem.at[1]),
    ]
    head_copies = [
        pltpu.make_async_copy(
            head_ref.at[pl.ds(i * QUART, QUART)], head.at[pl.ds(i * QUART, QUART)], head_sem.at[i]
        )
        for i in range(4)
    ]
    gains = (near_a, near_b, near_c, near_d)
    row_copies += [
        pltpu.make_async_copy(src, dst, own_sem.at[9 + j])
        for j, (src, dst) in enumerate(zip((gain_a, gain_b, gain_c, gain_d), gains))
    ]
    for copy in row_copies:
        copy.start()

    barrier = pltpu.get_barrier_semaphore()
    partners = [device(at, 1 - core)] + [
        device(along(at, axis, k), c) for axis in (2, 1, 0) for k in (1, 2, 3) for c in (0, 1)
    ]
    for partner in partners:
        pl.semaphore_signal(barrier, inc=1, device_id=partner, device_id_type=MESH)
    for copy in own_copies + head_copies:
        copy.start()

    for copy in row_copies:
        copy.wait()
    emb = xraw[z, 0, :, mine].astype(f32)
    hid = xraw[z, 1, :, mine].astype(f32)
    small[0, 0, 0] = jnp.concatenate(
        [
            jnp.sum(emb * emb, axis=0, keepdims=True),
            jnp.sum(hid * hid, axis=0, keepdims=True),
            jnp.concatenate(
                [
                    jnp.concatenate([g[...].astype(f32) for g in gains], axis=0),
                    jnp.zeros((4, ROWS - FEAT), f32),
                ],
                axis=1,
            ),
            jnp.zeros((2, ROWS), f32),
        ],
        axis=0,
    )
    pl.semaphore_wait(barrier, len(partners))

    def small_copy(phase, k, landed):
        blocks = [(0, 0, 0), (0, 0, pl.ds(0, 4)), (0, pl.ds(0, 4), pl.ds(0, 4))][phase]
        there = list(blocks)
        there[2 - phase] = 4 - k
        return pltpu.make_async_remote_copy(
            src_ref=small.at[tuple(there) if landed else blocks],
            dst_ref=small.at[tuple(there)],
            send_sem=small_s.at[phase * 3 + k - 1],
            recv_sem=small_r.at[phase * 3 + k - 1],
            device_id=device(along(at, 2 - phase, k), core),
            device_id_type=MESH,
        )

    def small_start(phase):
        waits.send([small_copy(phase, k, False) for k in (1, 3, 2)])

    def small_wait(phase):
        for k in (1, 3, 2):
            small_copy(phase, k, True).wait_recv()

    def x_copy(k, forward):
        to = ((core + 1) % 2) if forward or k == 0 else core
        ref = xraw.at[(z + 4 - k) % 4 if forward else z, :, :, mine]
        index = k + 3 if forward else k
        return pltpu.make_async_remote_copy(
            src_ref=ref,
            dst_ref=ref,
            send_sem=x_s.at[index],
            recv_sem=x_r.at[index],
            device_id=device(at if forward else along(at, 2, k), to),
            device_id_type=MESH,
        )

    def x_wait(k, forward):
        other = pl.ds(pl.multiple_of((1 - core) * ROWS, 128), ROWS)
        ref = xraw.at[(z + 4 - k) % 4, :, :, other if forward or k == 0 else mine]
        index = k + 3 if forward else k
        pltpu.make_async_remote_copy(
            src_ref=ref,
            dst_ref=ref,
            send_sem=x_s.at[index],
            recv_sem=x_r.at[index],
            device_id=device(at, 1 - core),
            device_id_type=MESH,
        ).wait_recv()

    def x_arrive():
        for k in (1, 3, 2):
            x_wait(k, False)
            waits.send([x_copy(k, True)])

    def x_all():
        for k in (1, 3, 2):
            x_wait(k, True)
        x_wait(0, False)

    small_start(0)
    waits.send([x_copy(k, False) for k in (1, 3, 2, 0)])
    waits.expect("x", x_arrive)
    waits.expect("x forwarded", x_all)

    ha, hb, hc = [
        Gather(
            waits,
            "h%d" % p,
            lambda s, r=r, n=n, c=c, m=m: gath.at[s + (pl.ds(r, n), pl.ds(c, m))],
            order,
            h_s,
            h_r,
            21 * p,
        )
        for p, (order, (r, n, c, m)) in enumerate(zip(H_ORDERS, H_PARTS))
    ]
    w_pairs = ((pe_ref, we), (ph_ref, wh))

    def w_copy(k, j, p, src, dst):
        return pltpu.make_async_remote_copy(
            src_ref=src,
            dst_ref=dst,
            send_sem=w_s.at[j, p * 3 + k - 1],
            recv_sem=w_r.at[j, p * 3 + k - 1],
            device_id=device(along(at, 2, k), core),
            device_id_type=MESH,
        )

    def w_start(p):
        c, n = PIECES[p]
        for k in (1, 3, 2):
            there = pl.ds(pl.multiple_of((z + k) % 4 * QUART + core * HALF + c, 128), n)
            waits.send(
                [
                    w_copy(k, j, p, src.at[:, there], dst.at[z, :, pl.ds(c, n)])
                    for j, (src, dst) in enumerate(w_pairs)
                ]
            )

        def w_wait(ks):
            for k in ks:
                for j, (_, dst) in enumerate(w_pairs):
                    ref = dst.at[(z + 4 - k) % 4, :, pl.ds(c, n)]
                    w_copy(k, j, p, ref, ref).wait_recv()

        waits.expect("w%dnear" % p, lambda: w_wait((1, 3)))
        waits.expect("w%d" % p, lambda: w_wait((2,)))

    small_wait(0)
    small_start(1)
    hc.start("0a", "0b")
    waits.receive("x")
    w_start(0)
    w_start(1)
    small_wait(1)
    small_start(2)
    for zr in (1, 2, 3):
        gath[0, 0, zr, :H_EARLY] = xraw[(z + zr) % 4, 1, :H_EARLY, mine]
    ha.start("Lb")
    hb.start("Lb")
    hc.wait("0a")
    hc.start("1b")
    ha.start("Lc")
    hb.start("Lc")
    small_wait(2)

    xsq[core] = jnp.sum(small[...].reshape(64, 8, ROWS), axis=0)

    def xsq_copy(which):
        ref = xsq.at[which]
        return pltpu.make_async_remote_copy(
            src_ref=ref,
            dst_ref=ref,
            send_sem=x_s.at[7],
            recv_sem=x_r.at[7],
            device_id=device(at, 1 - core),
            device_id_type=MESH,
        )

    waits.send([xsq_copy(core)])
    waits.expect("xsq", xsq_copy(1 - core).wait_recv)

    ha.wait("Lb")
    ha.start("Pc")
    hb.wait("Lb")
    hb.start("Pc")

    waits.receive("x forwarded")
    waits.receive("xsq")
    hid_scale = lax.rsqrt(xsq[core, 1:2] / D + epsilon)
    scales = [
        lax.rsqrt(jnp.concatenate([xsq[0, j : j + 1], xsq[1, j : j + 1]], axis=1) / D + epsilon) for j in (0, 1)
    ]
    for zr in range(4):
        block_gains = small[0, 0, zr, :, :128].T
        there = (z + zr) % 4
        for j, buf in enumerate((xe, xh)):
            raw = xraw[there, j].astype(f32)
            buf[there] = (raw * scales[j] * block_gains[:FEAT, 5 - j : 6 - j]).astype(bf16)
    for copy in own_copies:
        copy.wait()
    draft_gain = jnp.concatenate(
        [
            small[(z + 4 - x) % 4, (yy + 4 - y) % 4, (zz + 4 - z) % 4, 2:3, :FEAT]
            for yy in range(4)
            for zz in range(4)
        ],
        axis=1,
    )
    token = turn(token_ref[...].astype(f32))
    base = (lax.axis_index("vocab") * VOC).astype(f32)

    line = [(k, dc) for k in range(4) for dc in (0, 1)][1:]

    def r1_copy(p, half, k):
        lanes = pl.ds(*PIECES[p])
        to = (at[half] + k) % 4
        src = part.at[to, :, :, 0, :, lanes] if half == 0 else part.at[:, to, :, 1, :, lanes]
        return pltpu.make_async_remote_copy(
            src_ref=src,
            dst_ref=got1.at[half, k - 1, :, :, :, lanes],
            send_sem=r1_s.at[p * 6 + half * 3 + k - 1],
            recv_sem=r1_r.at[p * 6 + half * 3 + k - 1],
            device_id=device(along(at, half, k), core),
            device_id_type=MESH,
        )

    def r2_copy(p, half, k, dc):
        lanes = pl.ds(*PIECES[p])
        to = (core + dc) % 2
        axis = 1 - half
        return pltpu.make_async_remote_copy(
            src_ref=sum1.at[half, (at[axis] + k) % 4, to, :, lanes],
            dst_ref=got2.at[half, k * 2 + dc, :, lanes],
            send_sem=r2_s.at[p * 16 + half * 8 + k * 2 + dc],
            recv_sem=r2_r.at[p * 16 + half * 8 + k * 2 + dc],
            device_id=device(along(at, axis, k), to),
            device_id_type=MESH,
        )

    for p, (c0, n) in enumerate(PIECES):
        lanes = pl.ds(c0, n)
        waits.receive("w%dnear" % p)
        waits.receive("w%d" % p)
        for c in (0, 1):
            reqs = pl.ds(c * ROWS, ROWS)
            rows = lax.dot_general(
                xe[:, :, reqs].reshape(4 * FEAT, ROWS), we[:, :, lanes].reshape(4 * FEAT, n), FIRST,
                preferred_element_type=f32,
            ) + lax.dot_general(
                xh[:, :, reqs].reshape(4 * FEAT, ROWS), wh[:, :, lanes].reshape(4 * FEAT, n), FIRST,
                preferred_element_type=f32,
            )
            part[:, :, c, :, :, lanes] = rows.reshape(4, 4, 2, 8, n)
        for half in (0, 1):
            for k in (1, 3, 2):
                waits.send([r1_copy(p, half, k)])
                waits.expect("r1%d%d%d" % (p, half, k), r1_copy(p, half, k).wait_recv)
    hc.wait("0b", "1b")
    hc.start("Sc")
    for p, (c0, n) in enumerate(PIECES):
        lanes = pl.ds(c0, n)
        for half in (0, 1):
            own = part[x, :, :, 0, :, lanes] if half == 0 else part[:, y, :, 1, :, lanes]
            for k in (1, 3, 2):
                waits.receive("r1%d%d%d" % (p, half, k))
                own = own + got1[half, k - 1, :, :, :, lanes]
            sum1[half, :, :, :, lanes] = own
            for k, dc in line:
                waits.send([r2_copy(p, half, k, dc)])
                waits.expect("r2%d%d%d%d" % (p, half, k, dc), r2_copy(p, half, k, dc).wait_recv)

    state_halves = []
    for half in (0, 1):
        for p in (0, 1):
            for k, dc in line:
                waits.receive("r2%d%d%d%d" % (p, half, k, dc))
        same = sum1[half, at[1 - half], core]
        for k in (1, 2, 3):
            same = same + got2[half, k * 2]
        other = got2[half, 1] + got2[half, 3] + got2[half, 5] + got2[half, 7]
        state_halves.append(
            jnp.concatenate(
                [jnp.where(core == 0, same, other), jnp.where(core == 0, other, same)], axis=1
            )
        )
    state = jnp.concatenate(state_halves, axis=0)
    sq[z] = jnp.broadcast_to(jnp.sum(state * state, axis=1, keepdims=True), (16, 128))

    def q_copy(k, source):
        ref = sq.at[source]
        return pltpu.make_async_remote_copy(
            src_ref=ref,
            dst_ref=ref,
            send_sem=q_s.at[k - 1],
            recv_sem=q_r.at[k - 1],
            device_id=device(along(at, 2, k), core),
            device_id_type=MESH,
        )

    waits.send([q_copy(k, z) for k in (1, 3, 2)])
    for k in (1, 3, 2):
        waits.expect("q%d" % k, q_copy(k, (z + 4 - k) % 4).wait_recv)
    for copy in head_copies:
        copy.wait()
    for k in (1, 3, 2):
        waits.receive("q%d" % k)
    total = jnp.sum(sq[...], axis=0)[:, :1]
    gd[0, 0, 0] = (state * lax.rsqrt(total / D + epsilon) * draft_gain).astype(bf16)

    earlier = list(waits.sends)
    gs = [
        Gather(waits, "g%d" % p, lambda s, c=c, n=n: gd.at[s + (slice(None), pl.ds(c, n))], order, g_s, g_r, 21 * p)
        for p, (order, (c, n)) in enumerate(zip(G_ORDERS, G_PARTS))
    ]
    for g in gs:
        g.start("0a")
    def main_dot(q):
        rows = lax.dot_general(
            normed[q].reshape(QUART, ROWS), head[pl.ds(q * QUART, QUART)], FIRST, preferred_element_type=f32
        )
        main_ref[...] = rows if q == 0 else main_ref[...] + rows

    for g in gs:
        g.wait("0a")
        g.start("Lb")
    for g in gs:
        g.start("Lc")
    for g in gs:
        g.wait("Lb")
        g.start("Pc")
    ha.wait("Lc", "Pc")
    hb.wait("Lc", "Pc")
    hc.wait("Sc")

    def norm(xr, _):
        gain = small[xr].reshape(16, 8, ROWS)[:, 3, :128].T
        for yr in range(4):
            for zr in range(4):
                block = gath[xr, yr, zr].astype(f32) * hid_scale * gain[:FEAT, yr * 4 + zr : yr * 4 + zr + 1]
                normed[(x + xr) % 4, (y + yr) % 4, (z + zr) % 4] = block.astype(bf16)
        return 0

    lax.fori_loop(0, 4, norm, 0)
    main_dot(0)
    main_dot(1)
    main_dot(2)
    main_dot(3)

    def local_stats(ref):
        logits = ref[...]
        top = jnp.max(logits, axis=1, keepdims=True)
        return top, jnp.sum(jnp.exp(logits - top), axis=1, keepdims=True)

    main_out = pltpu.make_async_copy(main_ref, main_hbm, own_sem.at[7])
    main_out.start()
    main_top, main_sum = local_stats(main_ref)
    column = lax.broadcasted_iota(jnp.int32, (ROWS, VOC), 1).astype(f32) + base
    picked = jnp.sum(jnp.where(column == token[:, :1], main_ref[...], 0.0), axis=1, keepdims=True)

    def pack(values):
        lane = lax.broadcasted_iota(jnp.int32, (ROWS, 128), 1)
        packed = jnp.zeros((ROWS, 128), f32)
        for i, value in enumerate(values):
            packed = jnp.where(lane == i, value, packed)
        return packed.T[:8]

    def st_copy(which, phase, k, source):
        ref = stats.at[which, phase, source]
        index = which * 9 + phase * 3 + k - 1
        return pltpu.make_async_remote_copy(
            src_ref=ref,
            dst_ref=ref,
            send_sem=st_s.at[index],
            recv_sem=st_r.at[index],
            device_id=device(along(at, 2 - phase, k), core),
            device_id_type=MESH,
        )

    def st_start(which, phase, block):
        here = at[2 - phase]
        stats[which, phase, here] = block
        waits.send([st_copy(which, phase, k, here) for k in (1, 3, 2)])
        for k in (1, 3, 2):
            source = (here + 4 - k) % 4
            waits.expect("st%d%d%d" % (which, phase, k), st_copy(which, phase, k, source).wait_recv)

    def st_finish(which, phase):
        for k in (1, 3, 2):
            waits.receive("st%d%d%d" % (which, phase, k))
        got = stats[which, phase]
        tops = got[:, 0]
        top = jnp.max(tops, axis=0, keepdims=True)
        total = jnp.sum(got[:, 1] * jnp.exp(tops - top), axis=0, keepdims=True)
        pick = jnp.sum(got[:, 2], axis=0, keepdims=True)
        return jnp.concatenate([top, total, pick, jnp.zeros((5, ROWS), f32)], axis=0)

    st_start(0, 0, pack((main_top, main_sum, picked)))
    for copy in earlier:
        copy.wait_send()
    waits.sends = waits.sends[len(earlier) :]

    def draft_dot(p):
        c, n = G_PARTS[p]
        rows = None
        for zr in range(4):
            there = pl.ds(pl.multiple_of((z + zr) % 4 * QUART + c, 128), n)
            term = jnp.dot(
                gd[:, :, zr, :, c : c + n].reshape(ROWS, n), head[there], preferred_element_type=f32
            )
            rows = term if rows is None else rows + term
        return rows

    gs[2].wait("Lc", "Pc")
    acc[...] = draft_dot(2)
    st_start(0, 1, st_finish(0, 0))
    gs[0].wait("Lc", "Pc")
    acc[...] += draft_dot(0)
    gs[1].wait("Lc", "Pc")
    acc[...] += draft_dot(1)
    for xr in range(4):
        for yr in range(4):
            to = ((x + xr) % 4) * 4 + (y + yr) % 4
            draft_ref[pl.ds(pl.multiple_of(to * 16, 16), 16)] = acc[pl.ds((xr * 4 + yr) * 16, 16)]
    draft_out = pltpu.make_async_copy(draft_ref, draft_hbm, own_sem.at[8])
    draft_out.start()
    draft_top, draft_sum = local_stats(draft_ref)
    st_start(1, 0, pack((draft_top, draft_sum)))
    st_start(0, 2, st_finish(0, 1))
    st_start(1, 1, st_finish(1, 0))
    main_all = st_finish(0, 2)
    main_lse = main_all[0:1] + jnp.log(main_all[1:2])
    main_lse_ref[...] = main_lse

    member = lax.broadcasted_iota(jnp.int32, (REQS, ROWS), 0) == request_ref[...]
    partial = jnp.sum(jnp.where(member, main_all[2:3] - main_lse, 0.0), axis=1, keepdims=True)
    score_buf[core] = jnp.broadcast_to(partial, (REQS, 128))

    def sc_copy(source):
        ref = score_buf.at[source]
        return pltpu.make_async_remote_copy(
            src_ref=ref,
            dst_ref=ref,
            send_sem=sc_s,
            recv_sem=sc_r,
            device_id=device(at, 1 - core),
            device_id_type=MESH,
        )

    waits.send([sc_copy(core)])
    st_start(1, 2, st_finish(1, 1))
    sc_copy(1 - core).wait_recv()
    score_ref[...] = (score_buf[0] + score_buf[1]).T[:1]
    draft_all = st_finish(1, 2)
    draft_lse_ref[...] = draft_all[0:1] + jnp.log(draft_all[1:2])
    main_out.wait()
    draft_out.wait()
    waits.finish()


def per_device(
    hidden,
    next_embedding,
    final_gain,
    hidden_gain,
    embed_gain,
    draft_gain,
    head_weight,
    proj_embed,
    proj_hidden,
    token_ids,
    row_request,
):
    vmem = pl.BlockSpec(memory_space=pltpu.VMEM)
    hbm = pl.BlockSpec(memory_space=pltpu.HBM)
    main, draft, main_lse, draft_lse, score = pl.pallas_call(
        kernel,
        name="heads",
        out_shape=(
            jax.ShapeDtypeStruct((ROWS, VOC), f32),
            jax.ShapeDtypeStruct((ROWS, VOC), f32),
            jax.ShapeDtypeStruct((1, ROWS), f32),
            jax.ShapeDtypeStruct((1, ROWS), f32),
            jax.ShapeDtypeStruct((1, REQS), f32),
        ),
        in_specs=[hbm] * 11,
        out_specs=(hbm,) * 2 + (vmem,) * 3,
        scratch_shapes=[
            pltpu.VMEM((ROWS, VOC), f32),
            pltpu.VMEM((ROWS, VOC), f32),
            pltpu.VMEM((1, FEAT), bf16),
            pltpu.VMEM((1, FEAT), bf16),
            pltpu.VMEM((1, FEAT), bf16),
            pltpu.VMEM((1, FEAT), bf16),
            pltpu.VMEM((1, ROWS), jnp.int32),
            pltpu.VMEM((1, ROWS), jnp.int32),
            pltpu.VMEM((D, VOC), bf16),
            pltpu.VMEM((4, 4, 4, 8, ROWS), f32),
            pltpu.VMEM((4, 4, 4, FEAT, ROWS), bf16),
            pltpu.VMEM((4, 4, 4, FEAT, ROWS), bf16),
            pltpu.VMEM((4, 2, FEAT, 2 * ROWS), bf16),
            pltpu.VMEM((2, 8, ROWS), f32),
            pltpu.VMEM((4, FEAT, 2 * ROWS), bf16),
            pltpu.VMEM((4, FEAT, 2 * ROWS), bf16),
            pltpu.VMEM((4, FEAT, HALF), bf16),
            pltpu.VMEM((4, FEAT, HALF), bf16),
            pltpu.VMEM((4, 4, 2, 2, 8, HALF), f32),
            pltpu.VMEM((2, 3, 4, 2, 8, HALF), f32),
            pltpu.VMEM((2, 4, 2, 8, HALF), f32),
            pltpu.VMEM((2, 8, 8, HALF), f32),
            pltpu.VMEM((4, 16, 128), f32),
            pltpu.VMEM((4, 4, 4, 16, QUART), bf16),
            pltpu.VMEM((ROWS, VOC), f32),
            pltpu.VMEM((2, 3, 4, 8, ROWS), f32),
            pltpu.VMEM((2, REQS, 128), f32),
            DMA((4,)),
            DMA((13,)),
            DMA((9,)),
            DMA((9,)),
            DMA((2, 6)),
            DMA((2, 6)),
            DMA((8,)),
            DMA((8,)),
            DMA((63,)),
            DMA((63,)),
            DMA((12,)),
            DMA((12,)),
            DMA((32,)),
            DMA((32,)),
            DMA((3,)),
            DMA((3,)),
            DMA((63,)),
            DMA((63,)),
            DMA((18,)),
            DMA((18,)),
            DMA,
            DMA,
        ],
        compiler_params=pltpu.CompilerParams(
            collective_id=0, has_side_effects=True, vmem_limit_bytes=58 * 2**20
        ),
        cost_estimate=pl.CostEstimate(flops=8_300_000_000, bytes_accessed=20_000_000, transcendentals=600_000),
    )(
        hidden.T,
        next_embedding.T,
        draft_gain[None, :],
        final_gain[None, :],
        hidden_gain[None, :],
        embed_gain[None, :],
        token_ids[None, :],
        row_request[None, :],
        head_weight,
        proj_embed,
        proj_hidden,
    )
    return (main - main_lse[0][:, None], draft - draft_lse[0][:, None], score[0])


def solution(mesh):
    return jax.shard_map(
        per_device,
        mesh=mesh,
        in_specs=(
            P("req", "vocab"),
            P("req", "vocab"),
            P("vocab"),
            P("vocab"),
            P("vocab"),
            P("vocab"),
            P(None, "vocab"),
            P("vocab", None),
            P("vocab", None),
            P("req"),
            P("req"),
        ),
        out_specs=(P("req", "vocab"), P("req", "vocab"), P()),
        check_vma=False,
    )
```
